256 devices in a mesh: band: 4 (over y), img: 64 (over z, x, core).
Axes of the slice: x: 4, y: 4, z: 8, core: 2. Of those that a mesh axis runs over, the one named last changes fastest.
Arguments:
- images: bfloat16 [4, 1024, 3328], P('band', 'img'), may hold values from -12 to 12
- references: bfloat16 [4, 256, 3328], P('band', 'img'), may hold values from -0.08 to 0.08
- noise_weight: float32 [4, 1664], P('band'), may hold values from 0.5 to 4
- masks: int32 [4, 128, 64, 49], P('band', 'img'), may hold values from 0 to 1, as said below
Outputs:
- weighted_sums: float32 [4, 256, 3328], P('band', 'img')
- weight_totals: float32 [256], P('img')
The draws below stay inside these ranges and needn't reach their ends.
Inputs may be any that keep to these rules, and one draw needn't show every extreme that they name: `masks`: each entry is 0 or 1; translation number 49 // 2 is kept in every band, image block and orientation block.
All inputs are finite; a program needn't handle non-finite values.
Results may differ from the reference program's by a relative error of at most 0.0065.
Values may be sent and summed in bfloat16 or wider, within the bound.
A program may use at most 64 MiB of HBM per device.

```python
import math
import jax
import jax.numpy as jnp
from jax import lax

COEF = 1664
BOX = 256
SIDE = 7
IMG_BLOCK = 8
ORIENT_DEV = 4
SHIFTS = 49
BANDS = 4
IMAGES = 1024
ORIENT = 256
IBLOCKS = 128
OWNERS = 64


def draw_both(key):
    base = jax.random.fold_in(key, 11)
    key_refs = jax.random.fold_in(base, 0)
    key_amplitude = jax.random.fold_in(base, 1)
    key_images = jax.random.fold_in(base, 2)
    key_common = jax.random.fold_in(base, 5)
    amplitude = jnp.exp(jax.random.uniform(key_amplitude, (1, ORIENT, 1), jnp.float32, math.log(0.6), math.log(1.6)))
    projections = jax.random.normal(key_refs, (BANDS, ORIENT, 2 * COEF), jnp.float32) * 0.009 * amplitude
    common = 0.4 * jax.random.normal(key_common, (BANDS, 1, 2 * COEF), jnp.float32)
    noise = 0.67 * jax.random.normal(key_images, (BANDS, IMAGES, 2 * COEF), jnp.float32)
    pictures = noise + common
    return (jnp.clip(pictures, -12.0, 12.0), jnp.clip(projections, -0.08, 0.08))


def draw_images(key, part):
    pictures, projections = draw_both(key)
    return pictures.astype(jnp.bfloat16)


def draw_references(key, part):
    pictures, projections = draw_both(key)
    return projections.astype(jnp.bfloat16)


def draw_masks(key, part):
    key_level, key_roll = jax.random.split(jax.random.fold_in(key, 23))
    shape = (BANDS, IBLOCKS, OWNERS, SHIFTS)
    level = jax.random.randint(key_level, (1, IBLOCKS, 1, 1), 30, 96)
    roll = jax.random.randint(key_roll, shape, 0, 100)
    keep = (roll < level).astype(jnp.int32)
    center = (jnp.arange(SHIFTS, dtype=jnp.int32) == SHIFTS // 2).astype(jnp.int32)
    return jnp.maximum(keep, center[None, None, None, :])


def shard_levels(key, shape, shards, low, largest):
    def one(dim, parts):
        draws = jax.random.uniform(jax.random.fold_in(jax.random.fold_in(key, 6), dim), (parts,), jnp.float32, low / len(shards), largest / len(shards))
        return jnp.repeat(jnp.exp(draws), shape[dim] // parts).reshape((-1,) + (1,) * (len(shape) - dim - 1))

    factor_of = one(*shards[0])
    for cut in shards[1:]:
        factor_of = factor_of * one(*cut)
    return factor_of


def setup_inputs(seed: int = 0) -> dict:
    keys = jax.random.split(jax.random.key(seed), 5)
    images = draw_images(jax.random.fold_in(keys[4], 71), 0)
    references = draw_references(jax.random.fold_in(keys[4], 71), 0)
    noise_weight = jnp.clip(jnp.exp(math.log(4.0) - 2.0794415 * jax.random.uniform(keys[2], (BANDS, COEF), jnp.float32) ** shard_levels(keys[2], (BANDS, COEF), ((0, 4),), -0.2, 0.2)), 0.5, 4.0)
    masks = draw_masks(jax.random.fold_in(keys[4], 71), 0)
    return dict(images=images, references=references, noise_weight=noise_weight, masks=masks)


PENALTY = 10000.0


def shift_angles(band, coef):
    index = jnp.arange(coef, dtype=jnp.int32)
    freq_x = (index * 37 + band * 11) % 257 - 128
    freq_y = (index * 61 + band * 29) % 129
    shift_ids = jnp.arange(SIDE * SIDE, dtype=jnp.int32)
    move_x = shift_ids // SIDE - SIDE // 2
    move_y = shift_ids % SIDE - SIDE // 2
    phase = (move_x[:, None] * freq_x[None, :] + move_y[:, None] * freq_y[None, :]).astype(jnp.float32)
    angle = phase * (2.0 * math.pi / BOX)
    return jnp.cos(angle), jnp.sin(angle)


def align(pictures, cosine, sine):
    coef = cosine.shape[1]
    real = pictures[:, :coef].astype(jnp.float32)[:, None, :]
    imag = pictures[:, coef:].astype(jnp.float32)[:, None, :]
    out_real = real * cosine[None] - imag * sine[None]
    out_imag = real * sine[None] + imag * cosine[None]
    joined = jnp.concatenate([out_real, out_imag], axis=2).astype(jnp.bfloat16)
    return joined.reshape(pictures.shape[0] * cosine.shape[0], 2 * coef)


def prepare(projections, weight):
    doubled = jnp.concatenate([weight, weight])
    values = projections.astype(jnp.float32)
    weighted = (values * doubled[None, :]).astype(jnp.bfloat16)
    norms = jnp.sum(values * values * doubled[None, :], axis=1)
    return weighted, norms


def penalty(mask_block, img_block, orient_dev):
    blocks, owners, shift_count = mask_block.shape
    dropped = PENALTY * (1 - mask_block).astype(jnp.float32)
    dropped = jnp.transpose(dropped, (0, 2, 1))
    dropped = jnp.broadcast_to(dropped[:, None, :, :, None], (blocks, img_block, shift_count, owners, orient_dev))
    return dropped.reshape(blocks * img_block * shift_count, owners * orient_dev)


def band_term(aligned, weighted, norms, dropped):
    cross = lax.dot_general(aligned, weighted, (((1,), (1,)), ((), ())), preferred_element_type=jnp.float32)
    return cross - 0.5 * norms[None, :] - dropped


def posterior(total, count):
    grid = total.reshape(count, -1)
    peak = jnp.max(grid, axis=1, keepdims=True)
    raised = jnp.exp(grid - peak)
    return (raised / jnp.sum(raised, axis=1, keepdims=True)).reshape(total.shape)


def reference(images, references, noise_weight, masks):
    bands = images.shape[0]
    coef = noise_weight.shape[1]
    tables = [shift_angles(number, coef) for number in range(bands)]
    prepared = [prepare(references[number], noise_weight[number]) for number in range(bands)]
    blocks = images.shape[1] // IMG_BLOCK

    def one_block(carry, index):
        sums, totals = carry
        first = (index * IMG_BLOCK).astype(jnp.int32)
        kept = []
        score = jnp.zeros((IMG_BLOCK * SIDE * SIDE, ORIENT), jnp.float32)
        for number in range(bands):
            pictures = lax.dynamic_slice_in_dim(images[number], first, IMG_BLOCK, 0)
            current = align(pictures, tables[number][0], tables[number][1])
            mask_rows = lax.dynamic_slice_in_dim(masks[number], index.astype(jnp.int32), 1, 0)
            dropped = penalty(mask_rows, IMG_BLOCK, ORIENT_DEV)
            score = score + band_term(current, prepared[number][0], prepared[number][1], dropped)
            kept.append(current)
        prob = posterior(score, IMG_BLOCK)
        post = prob.astype(jnp.bfloat16)
        updated = []
        for number in range(bands):
            added = lax.dot_general(post, kept[number], (((0,), (0,)), ((), ())), preferred_element_type=jnp.float32)
            updated.append(sums[number] + added)
        totals = totals + jnp.sum(prob, axis=0)
        return (jnp.stack(updated), totals), None

    start_sums = jnp.zeros((bands, ORIENT, 2 * coef), jnp.float32)
    start_totals = jnp.zeros((ORIENT,), jnp.float32)
    (sums, totals), _ = lax.scan(one_block, (start_sums, start_totals), jnp.arange(blocks, dtype=jnp.int32))
    return sums, totals
```

```python
import functools
import math

import jax
import jax.numpy as jnp
import numpy as np
from jax import lax
from jax.experimental import pallas as pl
from jax.experimental.pallas import tpu as pltpu
from jax.sharding import PartitionSpec as P

BOX = 256
SIDE = 7
HALF = SIDE // 2
PENALTY = 10000.0
BANDS = 4
COEF = 1664
TILES = COEF // 128
SPLIT = 7
PACK = SPLIT * 128
MASKW = 512
BLOCK = 2 * COEF + MASKW
ROWS = 32 * SIDE
F32 = jnp.float32
BF16 = jnp.bfloat16


def trig_tables():
    index = np.arange(COEF)
    out = np.zeros((2 * BANDS, 8, COEF), np.float32)
    for band in range(BANDS):
        freqs = ((37 * index + 11 * band) % 257 - 128, (61 * index + 29 * band) % 129)
        for axis, freq in enumerate(freqs):
            for d in range(1, HALF + 1):
                angle = ((d * freq) % BOX) * (2.0 * math.pi / BOX)
                out[4 * axis + band, 2 * d - 2] = np.cos(angle)
                out[4 * axis + band, 2 * d - 1] = np.sin(angle)
    return out


def mod(a, n):
    return lax.rem(a + 4 * n, n)


def remote(src, dst, send, recv, device):
    return pltpu.make_async_remote_copy(
        src_ref=src,
        dst_ref=dst,
        send_sem=send,
        recv_sem=recv,
        device_id=device,
        device_id_type=pl.DeviceIdType.MESH,
    )


def nt_dot(a, b):
    return lax.dot_general(a, b, (((1,), (1,)), ((), ())), preferred_element_type=F32)


def kernel(
    images_ref, refs_ref, noise_ref, masks_ref, tab_hbm,
    out_ref, tot_ref,
    tab, stage, mcat, imgbuf, wpack, rbuf, xbuf, wbuf, sbuf, post, zbuf, obuf, cbuf, fbuf,
    tab_sem, tsend, trecv, rsend, rrecv, lsend, lrecv, wsend, wrecv, fsend, frecv,
    zsend, zrecv, csend, crecv, osend, orecv,
):
    y = lax.axis_index("band")
    m = lax.axis_index("img")
    core = lax.rem(m, 2)
    x = lax.rem(m // 2, 4)
    z = m // 8

    def dev(y, z, x, c):
        return (y, (z * 4 + x) * 2 + c)

    to_y = lax.rem(z, 4)
    to_z = mod(z + mod(y - to_y + 1, 4) - 1, 8)
    my_band = lax.rem(z, 4)

    def origin(slot):
        return mod(slot - (mod(lax.rem(slot, 4) - y + 1, 4) - 1), 8)

    moved = to_y != y
    target = dev(to_y, to_z, x, core)
    source = dev(my_band, origin(z), x, core)
    partner = dev(y, z, x, 1 - core)
    zright = dev(y, mod(z + 1, 8), x, core)
    zleft = dev(y, mod(z - 1, 8), x, core)

    def plane(k):
        return mod(y + k // 4, 4), mod(x + lax.rem(k, 4), 4)

    def plane_from(k):
        return mod(y - k // 4, 4), mod(x - lax.rem(k, 4), 4)

    barrier = pltpu.get_barrier_semaphore()

    def signal(device):
        pl.semaphore_signal(barrier, inc=1, device_id=device, device_id_type=pl.DeviceIdType.MESH)

    tab_copy = pltpu.make_async_copy(tab_hbm, tab, tab_sem)
    tab_copy.start()

    @pl.when(moved)
    def _():
        signal(target)

    apart = mod(y - to_y, 4) == 2

    @pl.when(apart)
    def _():
        signal(source)

    signal(partner)

    @pl.loop(1, 8)
    def _(d):
        signal(dev(y, mod(z + d, 8), x, core))

    @pl.loop(1, 16)
    def _(k):
        py, px = plane(k)
        signal(dev(py, z, px, core))

    mcat[...] = jnp.zeros_like(mcat)
    for s in range(SIDE * SIDE):
        dx, dy = s // SIDE, s % SIDE
        mcat[2 * dx : 2 * dx + 2, dy * 64 : dy * 64 + 64] = masks_ref[s].astype(F32)
    stage[:, : 2 * COEF] = images_ref[...]
    stage[:, 2 * COEF :] = mcat[...].astype(BF16)

    values = refs_ref[...].astype(F32)
    weight = noise_ref[...]
    re, im = values[:, :COEF], values[:, COEF:]
    wre, wim = re * weight, im * weight
    norm = jnp.sum(re * wre + im * wim, axis=1, keepdims=True)
    hi = norm.astype(BF16).astype(F32)
    mid = (norm - hi).astype(BF16).astype(F32)
    low = norm - hi - mid
    lane4 = lax.broadcasted_iota(jnp.int32, (4, 128), 1)
    spare = jnp.where(lane4 == 0, hi, jnp.where(lane4 == 1, mid, jnp.where(lane4 == 2, low, 0.0)))
    wpack[0:4, :] = wre[:, :PACK]
    wpack[4:8, :] = wim[:, :PACK]
    wpack[8:12, : COEF - PACK] = wre[:, PACK:]
    wpack[12:16, : COEF - PACK] = wim[:, PACK:]
    wpack[8:12, COEF - PACK :] = spare
    wpack[12:16, COEF - PACK :] = jnp.zeros((4, 128), F32)
    rbuf[y, x, core] = wpack[...].astype(BF16)

    pl.semaphore_wait(barrier, 23 + moved.astype(jnp.int32) + apart.astype(jnp.int32))

    @pl.when(moved)
    def _():
        remote(stage, imgbuf.at[to_z], tsend, trecv, target).start()

    @pl.when(jnp.logical_not(moved))
    def _():
        imgbuf[z] = stage[...]

    def refs_copy(k):
        py, px = plane(k)
        return remote(rbuf.at[y, x, core], rbuf.at[y, x, core], wsend.at[k], wrecv.at[k], dev(py, z, px, core))

    def refs_arrival(k):
        py, px = plane_from(k)
        return remote(rbuf.at[py, px, core], rbuf.at[py, px, core], wsend.at[k], wrecv.at[k], dev(py, z, px, core))

    def refs_forward(k):
        py, px = plane_from(k)
        return remote(rbuf.at[py, px, core], rbuf.at[py, px, core], fsend.at[k], frecv.at[k], partner)

    def refs_forwarded(k):
        py, px = plane_from(k)
        return remote(rbuf.at[py, px, 1 - core], rbuf.at[py, px, 1 - core], fsend.at[k], frecv.at[k], partner)

    @pl.loop(1, 16)
    def _(k):
        refs_copy(k).start()

    refs_forward(0).start()

    @pl.when(moved)
    def _():
        remote(stage, imgbuf.at[z], tsend, trecv, source).wait_recv()

    def ring_right(step):
        slot = mod(z - (step - 1), 8)
        ref = imgbuf.at[slot] if step < 4 else imgbuf.at[slot, :, pl.ds(0, BLOCK // 2)]
        return remote(ref, ref, rsend.at[step - 1], rrecv.at[step - 1], zright)

    def ring_left(step):
        slot = mod(z + (step - 1), 8)
        ref = imgbuf.at[slot] if step < 4 else imgbuf.at[slot, :, pl.ds(BLOCK // 2, BLOCK // 2)]
        return remote(ref, ref, lsend.at[step - 1], lrecv.at[step - 1], zleft)

    def ring_arrive(step):
        slot = mod(z - step, 8)
        ref = imgbuf.at[slot] if step < 4 else imgbuf.at[slot, :, pl.ds(0, BLOCK // 2)]
        remote(ref, ref, rsend.at[step - 1], rrecv.at[step - 1], zright).wait_recv()
        slot = mod(z + step, 8)
        ref = imgbuf.at[slot] if step < 4 else imgbuf.at[slot, :, pl.ds(BLOCK // 2, BLOCK // 2)]
        remote(ref, ref, lsend.at[step - 1], lrecv.at[step - 1], zleft).wait_recv()

    def ring_start(step):
        ring_right(step).start()
        ring_left(step).start()

    ring_start(1)
    tab_copy.wait()

    def shifted(re, im, table, d):
        c, s = table[2 * d - 2 : 2 * d - 1], table[2 * d - 1 : 2 * d]
        a, b, g, h = re * c, im * s, re * s, im * c
        return (a - b, g + h), (a + b, h - g)

    def prepare_images(slot):
        band = lax.rem(slot, 4)
        first = (origin(slot) // 4) * 16

        def rows(n):
            return pl.ds(pl.multiple_of((HALF + n) * 32 + first, 16), 16)

        @pl.loop(0, TILES)
        def _(t):
            lanes = pl.ds(pl.multiple_of(t * 128, 128), 128)
            lanes_im = pl.ds(pl.multiple_of(t * 128 + COEF, 128), 128)
            out_re = pl.ds(pl.multiple_of(t * 256, 128), 128)
            out_im = pl.ds(pl.multiple_of(t * 256 + 128, 128), 128)
            raw_re, raw_im = imgbuf[slot, :, lanes], imgbuf[slot, :, lanes_im]
            xbuf[band, rows(0), out_re] = raw_re
            xbuf[band, rows(0), out_im] = raw_im
            re, im = raw_re.astype(F32), raw_im.astype(F32)
            table = tab[band, :, lanes]
            for d in range(1, HALF + 1):
                up, down = shifted(re, im, table, d)
                xbuf[band, rows(d), out_re] = up[0].astype(BF16)
                xbuf[band, rows(d), out_im] = up[1].astype(BF16)
                xbuf[band, rows(-d), out_re] = down[0].astype(BF16)
                xbuf[band, rows(-d), out_im] = down[1].astype(BF16)

    def prepare_refs(band):
        def store(t, re, im):
            lanes = pl.ds(pl.multiple_of(t * 128, 128), 128)
            out_re = pl.ds(pl.multiple_of(t * 256, 128), 128)
            out_im = pl.ds(pl.multiple_of(t * 256 + 128, 128), 128)
            table = tab[BANDS + band, :, lanes]

            def put(n, pair):
                wbuf[band, (HALF + n) * 32 : (HALF + n) * 32 + 32, out_re] = pair[0].astype(BF16)
                wbuf[band, (HALF + n) * 32 : (HALF + n) * 32 + 32, out_im] = pair[1].astype(BF16)

            put(0, (re, im))
            for d in range(1, HALF + 1):
                up, down = shifted(re, im, table, d)
                put(-d, up)
                put(d, down)

        def load(t):
            lanes = pl.ds(pl.multiple_of(t * 128, 128), 128)
            blocks = [rbuf[band, xx, cc, :, lanes].astype(F32) for xx in range(4) for cc in range(2)]
            return [jnp.concatenate([b[4 * q : 4 * q + 4] for b in blocks], axis=0) for q in range(4)]

        @pl.loop(0, SPLIT - 1)
        def _(t):
            re, im, re2, im2 = load(t)
            store(t, re, im)
            store(t + SPLIT, re2, im2)

        re, im, spare, _ = load(SPLIT - 1)
        store(SPLIT - 1, re, im)
        return spare

    def score_band(band, first):
        term = nt_dot(xbuf[band], wbuf[band])
        if first:
            sbuf[...] = term
        else:
            sbuf[...] += term

    prepare_images(z)
    ring_arrive(1)
    ring_start(2)

    @pl.loop(1, 16)
    def _(k):
        refs_arrival(k).wait_recv()
        refs_forward(k).start()

    prepare_images(mod(z - 1, 8))
    prepare_images(mod(z + 1, 8))

    ring_arrive(2)
    ring_start(3)

    @pl.loop(0, 16)
    def _(k):
        refs_forwarded(k).wait_recv()

    half = jnp.where(lax.broadcasted_iota(jnp.int32, (8, 128), 1) < 3, -0.5, 0.0).astype(BF16)
    norms = jnp.zeros((8, 32), F32)
    for band in range(BANDS):
        norms += nt_dot(half, prepare_refs(band).astype(BF16))
    norms = jnp.concatenate([norms] * SIDE, axis=1)

    prepare_images(mod(z - 2, 8))
    prepare_images(mod(z + 2, 8))
    score_band(mod(z + 2, 4), True)

    ring_arrive(3)
    ring_start(4)
    prepare_images(mod(z - 3, 8))
    prepare_images(mod(z + 3, 8))
    score_band(mod(z + 1, 4), False)
    score_band(mod(z + 3, 4), False)
    row = lax.broadcasted_iota(jnp.int32, (MASKW, ROWS), 0)
    lane = lax.broadcasted_iota(jnp.int32, (MASKW, ROWS), 1)
    spread = jnp.where(row == (lane >> 5) * 64 + 8 * z + ((lane & 31) >> 2), 1.0, 0.0).astype(BF16)

    ring_arrive(4)
    prepare_images(mod(z + 4, 8))
    score_band(lax.rem(z, 4), False)

    kept = []
    for e in range(2):
        total = jnp.zeros((16, MASKW), F32)
        for band in range(BANDS):
            slot = mod(y + 4 * e + mod(band - y + 1, 4) - 1, 8)
            total += imgbuf[slot, :, 2 * COEF :].astype(F32)
        kept.append(lax.dot_general(total.astype(BF16), spread, (((1,), (0,)), ((), ())), preferred_element_type=F32))

    lane8 = lax.broadcasted_iota(jnp.int32, (8, 128), 1)
    message = jnp.zeros((8, 128), F32)
    for q in range(4):
        e, block = q // 2, q % 2
        tiles = []
        for dx in range(SIDE):
            line = kept[e][2 * dx + block : 2 * dx + block + 1]
            tiles.append(sbuf[dx * 32 + q * 8 : dx * 32 + q * 8 + 8, :] + norms - PENALTY * (BANDS - line))
        peak = tiles[0]
        for tile in tiles[1:]:
            peak = jnp.maximum(peak, tile)
        peak = jnp.max(peak, axis=1, keepdims=True)
        mass = jnp.zeros((8, ROWS), F32)
        for dx in range(SIDE):
            raised = jnp.exp(tiles[dx] - peak)
            sbuf[dx * 32 + q * 8 : dx * 32 + q * 8 + 8, :] = raised
            mass += raised
        mass = jnp.sum(mass, axis=1, keepdims=True)
        message = jnp.where(lane8 == q, peak, jnp.where(lane8 == 4 + q, mass, message))
    zbuf[z] = message

    def z_copy(d):
        return remote(zbuf.at[z], zbuf.at[z], zsend.at[d], zrecv.at[d], dev(y, mod(z + d, 8), x, core))

    def z_arrival(d):
        slot = mod(z - d, 8)
        return remote(zbuf.at[slot], zbuf.at[slot], zsend.at[d], zrecv.at[d], dev(y, slot, x, core))

    @pl.loop(1, 8)
    def _(d):
        z_copy(d).start()

    @pl.loop(1, 8)
    def _(d):
        z_arrival(d).wait_recv()

    top = zbuf[0]
    for slot in range(1, 8):
        top = jnp.maximum(top, zbuf[slot])
    whole = jnp.zeros((8, 128), F32)
    for slot in range(8):
        part = zbuf[slot]
        whole += pltpu.roll(part, 124, 1) * jnp.exp(jnp.where(lane8 < 4, part - top, 0.0))
    factor = jnp.exp(jnp.where(lane8 < 4, message - top, 0.0)) / jnp.where(lane8 < 4, whole, 1.0)
    for q in range(4):
        scale = factor[:, q : q + 1]
        for dx in range(SIDE):
            sbuf[dx * 32 + q * 8 : dx * 32 + q * 8 + 8, :] = sbuf[dx * 32 + q * 8 : dx * 32 + q * 8 + 8, :] * scale
    prob = sbuf[...].T
    post[...] = prob.astype(BF16)
    mass = jnp.sum(prob, axis=1, keepdims=True)
    totals = mass[0:32]
    for dy in range(1, SIDE):
        totals += mass[dy * 32 : dy * 32 + 32]
    thi = totals.astype(BF16).astype(F32)
    lane32 = lax.broadcasted_iota(jnp.int32, (32, 128), 1)
    spare_re = jnp.where(lane32 == 0, thi, jnp.where(lane32 == 1, totals - thi, 0.0))
    spare_im = jnp.zeros((32, 128), F32)

    def sums_tile(band, t):
        lanes = pl.ds(pl.multiple_of(t * 128, 128), 128)
        both = pl.ds(pl.multiple_of(t * 256, 256), 256)
        g = jnp.dot(post[...], xbuf[band, :, both], preferred_element_type=F32)
        table = tab[BANDS + band, :, lanes]

        def part(n):
            r = (HALF + n) * 32
            return g[r : r + 32, :128], g[r : r + 32, 128:]

        re, im = part(0)
        for d in range(1, HALF + 1):
            c, s = table[2 * d - 2 : 2 * d - 1], table[2 * d - 1 : 2 * d]
            (ur, ui), (dr, di) = part(d), part(-d)
            re = re + c * (ur + dr) - s * (ui - di)
            im = im + s * (ur - dr) + c * (ui + di)
        return re, im

    def pack(band, t, upper, lower):
        lanes = pl.ds(pl.multiple_of(t * 128, 128), 128)
        for xx in range(4):
            for cc in range(2):
                r = xx * 8 + cc * 4
                rows = jnp.concatenate([a[r : r + 4] for a in (*upper, *lower)], axis=0)
                obuf[band, cc, xx, :, lanes] = rows.astype(BF16)

    def core_copy(k):
        band = mod(y + k, 4)
        return remote(obuf.at[band, 1 - core], cbuf.at[k], csend.at[k], crecv.at[k], partner)

    def out_copy(k):
        py, px = plane(k)
        return remote(obuf.at[py, core, px], fbuf.at[k], osend.at[k], orecv.at[k], dev(py, z, px, core))

    def sums_band(k):
        band = mod(y + k, 4)

        @pl.loop(0, SPLIT - 1)
        def _(t):
            pack(band, t, sums_tile(band, t), sums_tile(band, t + SPLIT))

        pack(band, SPLIT - 1, sums_tile(band, SPLIT - 1), (spare_re, spare_im))
        core_copy(k).start()

    def owners_band(k):
        band = mod(y + k, 4)
        core_copy(k).wait_recv()
        for xx in range(4):
            mine = obuf[band, core, xx].astype(F32) + cbuf[k, xx].astype(F32)
            obuf[band, core, xx] = mine.astype(BF16)
        for j in range(4):
            if (4 * k + j) % 16:
                out_copy(4 * k + j).start()

    sums_band(1)
    sums_band(2)
    owners_band(1)
    sums_band(3)
    owners_band(2)
    sums_band(0)
    owners_band(3)
    owners_band(0)

    @pl.loop(1, 16)
    def _(k):
        out_copy(k).wait_recv()

    final = obuf[y, core, x].astype(F32)
    for k in range(1, 16):
        final += fbuf[k].astype(F32)
    out_ref[:, :PACK] = final[0:4]
    out_ref[:, COEF : COEF + PACK] = final[4:8]
    out_ref[:, PACK:COEF] = final[8:12, : COEF - PACK]
    out_ref[:, COEF + PACK :] = final[12:16, : COEF - PACK]
    pair = final[8:12, COEF - PACK : COEF - PACK + 1] + final[8:12, COEF - PACK + 1 : COEF - PACK + 2]
    eye = lax.broadcasted_iota(jnp.int32, (4, 4), 0) == lax.broadcasted_iota(jnp.int32, (4, 4), 1)
    tot_ref[...] = jnp.sum(jnp.where(eye, pair, 0.0), axis=0, keepdims=True)

    @pl.when(moved)
    def _():
        remote(stage, imgbuf.at[to_z], tsend, trecv, target).wait_send()

    for step in range(1, 5):
        ring_right(step).wait_send()
        ring_left(step).wait_send()

    @pl.loop(1, 16)
    def _(k):
        refs_copy(k).wait_send()
        out_copy(k).wait_send()

    @pl.loop(0, 16)
    def _(k):
        refs_forward(k).wait_send()

    @pl.loop(1, 8)
    def _(d):
        z_copy(d).wait_send()

    @pl.loop(0, 4)
    def _(k):
        core_copy(k).wait_send()


def per_device(images, references, noise_weight, masks):
    vmem = pl.BlockSpec(memory_space=pltpu.VMEM)
    dma = pltpu.SemaphoreType.DMA
    sums, totals = pl.pallas_call(
        kernel,
        out_shape=(jax.ShapeDtypeStruct((4, 2 * COEF), F32), jax.ShapeDtypeStruct((1, 4), F32)),
        in_specs=[vmem, vmem, vmem, vmem, pl.BlockSpec(memory_space=pl.ANY)],
        out_specs=(vmem, vmem),
        scratch_shapes=[
            pltpu.VMEM((2 * BANDS, 8, COEF), F32),
            pltpu.VMEM((16, BLOCK), BF16),
            pltpu.VMEM((16, MASKW), F32),
            pltpu.VMEM((8, 16, BLOCK), BF16),
            pltpu.VMEM((16, PACK), F32),
            pltpu.VMEM((BANDS, 4, 2, 16, PACK), BF16),
            pltpu.VMEM((BANDS, ROWS, 2 * COEF), BF16),
            pltpu.VMEM((BANDS, ROWS, 2 * COEF), BF16),
            pltpu.VMEM((ROWS, ROWS), F32),
            pltpu.VMEM((ROWS, ROWS), BF16),
            pltpu.VMEM((8, 8, 128), F32),
            pltpu.VMEM((BANDS, 2, 4, 16, PACK), BF16),
            pltpu.VMEM((BANDS, 4, 16, PACK), BF16),
            pltpu.VMEM((16, 16, PACK), BF16),
            dma, dma, dma,
            dma((4,)), dma((4,)), dma((4,)), dma((4,)),
            dma((16,)), dma((16,)), dma((16,)), dma((16,)),
            dma((8,)), dma((8,)), dma((4,)), dma((4,)), dma((16,)), dma((16,)),
        ],
        compiler_params=pltpu.CompilerParams(
            collective_id=0, has_side_effects=True, vmem_limit_bytes=48 * 1024 * 1024
        ),
    )(
        images[0],
        references[0],
        noise_weight,
        jnp.transpose(masks[0], (2, 0, 1)),
        jnp.asarray(trig_tables()),
    )
    return sums[None], totals[0]


def solution(mesh):
    in_specs = (
        P("band", "img", None),
        P("band", "img", None),
        P("band", None),
        P("band", "img", None, None),
    )
    out_specs = (P("band", "img", None), P("img"))
    return jax.shard_map(
        per_device, mesh=mesh, in_specs=in_specs, out_specs=out_specs, check_vma=False
    )
```

```python
import functools
import math

import jax
import jax.numpy as jnp
import numpy as np
from jax import lax
from jax.experimental import pallas as pl
from jax.experimental.pallas import tpu as pltpu
from jax.sharding import PartitionSpec as P

BOX = 256
SIDE = 7
HALF = SIDE // 2
PENALTY = 10000.0
BANDS = 4
COEF = 1664
TILES = COEF // 128
SPLIT = 7
PACK = SPLIT * 128
MASKW = 512
BLOCK = 2 * COEF + MASKW
CHUNKS = ((0, 8), (8, 8), (16, 7), (23, 7))
ROWS = 32 * SIDE
F32 = jnp.float32
BF16 = jnp.bfloat16


def trig_tables():
    index = np.arange(COEF)
    out = np.zeros((2 * BANDS, 8, COEF), np.float32)
    for band in range(BANDS):
        freqs = ((37 * index + 11 * band) % 257 - 128, (61 * index + 29 * band) % 129)
        for axis, freq in enumerate(freqs):
            for d in range(1, HALF + 1):
                angle = ((d * freq) % BOX) * (2.0 * math.pi / BOX)
                out[4 * axis + band, 2 * d - 2] = np.cos(angle)
                out[4 * axis + band, 2 * d - 1] = np.sin(angle)
    return out


def mod(a, n):
    return lax.rem(a + 4 * n, n)


def remote(src, dst, send, recv, device):
    return pltpu.make_async_remote_copy(
        src_ref=src,
        dst_ref=dst,
        send_sem=send,
        recv_sem=recv,
        device_id=device,
        device_id_type=pl.DeviceIdType.MESH,
    )


def nt_dot(a, b):
    return lax.dot_general(a, b, (((1,), (1,)), ((), ())), preferred_element_type=F32)


def kernel(
    images_hbm, refs_hbm, noise_hbm, masks_hbm, tab_hbm,
    out_ref, tot_ref,
    refs_ref, noise_ref, masks_ref, tab, stage, mcat, imgbuf, wpack, rbuf, xbuf, wbuf, sbuf, post, zbuf, obuf, cbuf, fbuf,
    in_sem, tab_sem, tsend, trecv, rsend, rrecv, lsend, lrecv, wsend, wrecv, fsend, frecv,
    zsend, zrecv, csend, crecv, osend, orecv,
):
    y = lax.axis_index("band")
    m = lax.axis_index("img")
    core = lax.rem(m, 2)
    x = lax.rem(m // 2, 4)
    z = m // 8

    def dev(y, z, x, c):
        return (y, (z * 4 + x) * 2 + c)

    to_y = lax.rem(z, 4)
    to_z = mod(z + mod(y - to_y + 1, 4) - 1, 8)
    my_band = lax.rem(z, 4)

    def origin(slot):
        return mod(slot - (mod(lax.rem(slot, 4) - y + 1, 4) - 1), 8)

    moved = to_y != y
    target = dev(to_y, to_z, x, core)
    source = dev(my_band, origin(z), x, core)
    partner = dev(y, z, x, 1 - core)
    zright = dev(y, mod(z + 1, 8), x, core)
    zleft = dev(y, mod(z - 1, 8), x, core)

    def plane(k):
        return mod(y + k // 4, 4), mod(x + lax.rem(k, 4), 4)

    def plane_from(k):
        return mod(y - k // 4, 4), mod(x - lax.rem(k, 4), 4)

    barrier = pltpu.get_barrier_semaphore()

    def signal(device):
        pl.semaphore_signal(barrier, inc=1, device_id=device, device_id_type=pl.DeviceIdType.MESH)

    inputs = [
        pltpu.make_async_copy(refs_hbm, refs_ref, in_sem.at[0]),
        pltpu.make_async_copy(noise_hbm, noise_ref, in_sem.at[1]),
        pltpu.make_async_copy(masks_hbm, masks_ref, in_sem.at[2]),
    ]
    for copy in inputs:
        copy.start()
    tab_copy = pltpu.make_async_copy(tab_hbm, tab, tab_sem)
    tab_copy.start()

    @pl.when(moved)
    def _():
        signal(target)

    apart = mod(y - to_y, 4) == 2

    @pl.when(apart)
    def _():
        signal(source)

    signal(partner)

    @pl.loop(1, 8)
    def _(d):
        signal(dev(y, mod(z + d, 8), x, core))

    @pl.loop(1, 16)
    def _(k):
        py, px = plane(k)
        signal(dev(py, z, px, core))

    for copy in inputs:
        copy.wait()
    mcat[...] = jnp.zeros_like(mcat)
    for s in range(SIDE * SIDE):
        dx, dy = s // SIDE, s % SIDE
        mcat[2 * dx : 2 * dx + 2, dy * 64 : dy * 64 + 64] = masks_ref[s].astype(F32)
    stage[...] = mcat[...].astype(BF16)

    values = refs_ref[...].astype(F32)
    weight = noise_ref[...]
    re, im = values[:, :COEF], values[:, COEF:]
    wre, wim = re * weight, im * weight
    norm = jnp.sum(re * wre + im * wim, axis=1, keepdims=True)
    hi = norm.astype(BF16).astype(F32)
    mid = (norm - hi).astype(BF16).astype(F32)
    low = norm - hi - mid
    lane4 = lax.broadcasted_iota(jnp.int32, (4, 128), 1)
    spare = jnp.where(lane4 == 0, hi, jnp.where(lane4 == 1, mid, jnp.where(lane4 == 2, low, 0.0)))
    wpack[0:4, :] = wre[:, :PACK]
    wpack[4:8, :] = wim[:, :PACK]
    wpack[8:12, : COEF - PACK] = wre[:, PACK:]
    wpack[12:16, : COEF - PACK] = wim[:, PACK:]
    wpack[8:12, COEF - PACK :] = spare
    wpack[12:16, COEF - PACK :] = jnp.zeros((4, 128), F32)
    rbuf[y, x, core] = wpack[...].astype(BF16)

    pl.semaphore_wait(barrier, 23 + moved.astype(jnp.int32) + apart.astype(jnp.int32))

    def lanes_of(j):
        return pl.ds(CHUNKS[j][0] * 128, CHUNKS[j][1] * 128)

    def piece(j, slot):
        if j == 4:
            return stage, imgbuf.at[slot, :, pl.ds(2 * COEF, MASKW)]
        first = CHUNKS[j][0] * 128
        lanes = pl.ds(first, min(CHUNKS[j][1] * 128, 2 * COEF - first))
        return images_hbm.at[:, lanes], imgbuf.at[slot, :, lanes]

    def move(j):
        return remote(*piece(j, to_z), tsend.at[j], trecv.at[j], target)

    def moved_in(j):
        return remote(*piece(j, z), tsend.at[j], trecv.at[j], source)

    def keep(j):
        return pltpu.make_async_copy(*piece(j, z), tsend.at[j])

    @pl.when(moved)
    def _():
        for j in range(5):
            move(j).start()

    @pl.when(jnp.logical_not(moved))
    def _():
        for j in range(5):
            keep(j).start()

    def refs_copy(k):
        py, px = plane(k)
        return remote(rbuf.at[y, x, core], rbuf.at[y, x, core], wsend.at[k], wrecv.at[k], dev(py, z, px, core))

    def refs_arrival(k):
        py, px = plane_from(k)
        return remote(rbuf.at[py, px, core], rbuf.at[py, px, core], wsend.at[k], wrecv.at[k], dev(py, z, px, core))

    def refs_forward(k):
        py, px = plane_from(k)
        return remote(rbuf.at[py, px, core], rbuf.at[py, px, core], fsend.at[k], frecv.at[k], partner)

    def refs_forwarded(k):
        py, px = plane_from(k)
        return remote(rbuf.at[py, px, 1 - core], rbuf.at[py, px, 1 - core], fsend.at[k], frecv.at[k], partner)

    @pl.loop(1, 16)
    def _(k):
        refs_copy(k).start()

    refs_forward(0).start()

    RIGHT = [(0, 1, 2, 3)] * 3 + [(0, 1)]
    LEFT = [(0, 1, 2, 3)] * 3 + [(2, 3)]

    def ring_copy(slot, step, j, send, recv, device):
        ref = imgbuf.at[slot, :, lanes_of(j)]
        return remote(ref, ref, send.at[step - 1, j], recv.at[step - 1, j], device)

    def ring_right(step, j):
        return ring_copy(mod(z - (step - 1), 8), step, j, rsend, rrecv, zright)

    def ring_left(step, j):
        return ring_copy(mod(z + (step - 1), 8), step, j, lsend, lrecv, zleft)

    def ring_step(step):
        for j in range(4):
            if j in RIGHT[step - 1]:
                ring_copy(mod(z - step, 8), step, j, rsend, rrecv, zleft).wait_recv()
                if step < 4 and j in RIGHT[step]:
                    ring_right(step + 1, j).start()
            if j in LEFT[step - 1]:
                ring_copy(mod(z + step, 8), step, j, lsend, lrecv, zright).wait_recv()
                if step < 4 and j in LEFT[step]:
                    ring_left(step + 1, j).start()

    for j in range(4):
        for jj in (3, 4) if j == 3 else (j,):

            @pl.when(moved)
            def _():
                moved_in(jj).wait_recv()

            @pl.when(jnp.logical_not(moved))
            def _():
                keep(jj).wait()

        ring_right(1, j).start()
        ring_left(1, j).start()
    tab_copy.wait()

    def shifted(re, im, table, d):
        c, s = table[2 * d - 2 : 2 * d - 1], table[2 * d - 1 : 2 * d]
        a, b, g, h = re * c, im * s, re * s, im * c
        return (a - b, g + h), (a + b, h - g)

    def prepare_images(slot):
        band = lax.rem(slot, 4)
        first = (origin(slot) // 4) * 16

        def rows(n):
            return pl.ds(pl.multiple_of((HALF + n) * 32 + first, 16), 16)

        @pl.loop(0, TILES)
        def _(t):
            lanes = pl.ds(pl.multiple_of(t * 128, 128), 128)
            lanes_im = pl.ds(pl.multiple_of(t * 128 + COEF, 128), 128)
            out_re = pl.ds(pl.multiple_of(t * 256, 128), 128)
            out_im = pl.ds(pl.multiple_of(t * 256 + 128, 128), 128)
            raw_re, raw_im = imgbuf[slot, :, lanes], imgbuf[slot, :, lanes_im]
            xbuf[band, rows(0), out_re] = raw_re
            xbuf[band, rows(0), out_im] = raw_im
            re, im = raw_re.astype(F32), raw_im.astype(F32)
            table = tab[band, :, lanes]
            for d in range(1, HALF + 1):
                up, down = shifted(re, im, table, d)
                xbuf[band, rows(d), out_re] = up[0].astype(BF16)
                xbuf[band, rows(d), out_im] = up[1].astype(BF16)
                xbuf[band, rows(-d), out_re] = down[0].astype(BF16)
                xbuf[band, rows(-d), out_im] = down[1].astype(BF16)

    def prepare_refs(band):
        def store(t, re, im):
            lanes = pl.ds(pl.multiple_of(t * 128, 128), 128)
            out_re = pl.ds(pl.multiple_of(t * 256, 128), 128)
            out_im = pl.ds(pl.multiple_of(t * 256 + 128, 128), 128)
            table = tab[BANDS + band, :, lanes]

            def put(n, pair):
                wbuf[band, (HALF + n) * 32 : (HALF + n) * 32 + 32, out_re] = pair[0].astype(BF16)
                wbuf[band, (HALF + n) * 32 : (HALF + n) * 32 + 32, out_im] = pair[1].astype(BF16)

            put(0, (re, im))
            for d in range(1, HALF + 1):
                up, down = shifted(re, im, table, d)
                put(-d, up)
                put(d, down)

        def load(t):
            lanes = pl.ds(pl.multiple_of(t * 128, 128), 128)
            blocks = [rbuf[band, xx, cc, :, lanes].astype(F32) for xx in range(4) for cc in range(2)]
            return [jnp.concatenate([b[4 * q : 4 * q + 4] for b in blocks], axis=0) for q in range(4)]

        @pl.loop(0, SPLIT - 1)
        def _(t):
            re, im, re2, im2 = load(t)
            store(t, re, im)
            store(t + SPLIT, re2, im2)

        re, im, spare, _ = load(SPLIT - 1)
        store(SPLIT - 1, re, im)
        return spare

    def score_band(band, first):
        term = nt_dot(xbuf[band], wbuf[band])
        if first:
            sbuf[...] = term
        else:
            sbuf[...] += term

    prepare_images(z)
    ring_step(1)
    prepare_images(mod(z - 1, 8))
    prepare_images(mod(z + 1, 8))

    @pl.loop(1, 16)
    def _(k):
        refs_arrival(k).wait_recv()
        refs_forward(k).start()

    ring_step(2)
    prepare_images(mod(z - 2, 8))
    prepare_images(mod(z + 2, 8))

    @pl.loop(0, 16)
    def _(k):
        refs_forwarded(k).wait_recv()

    half = jnp.where(lax.broadcasted_iota(jnp.int32, (8, 128), 1) < 3, -0.5, 0.0).astype(BF16)
    norms = jnp.zeros((8, 32), F32)
    for band in range(BANDS):
        norms += nt_dot(half, prepare_refs(band).astype(BF16))
    norms = jnp.concatenate([norms] * SIDE, axis=1)
    score_band(mod(z + 2, 4), True)

    ring_step(3)
    prepare_images(mod(z - 3, 8))
    prepare_images(mod(z + 3, 8))
    score_band(mod(z + 1, 4), False)
    score_band(mod(z + 3, 4), False)
    row = lax.broadcasted_iota(jnp.int32, (MASKW, ROWS), 0)
    lane = lax.broadcasted_iota(jnp.int32, (MASKW, ROWS), 1)
    spread = jnp.where(row == (lane >> 5) * 64 + 8 * z + ((lane & 31) >> 2), 1.0, 0.0).astype(BF16)

    ring_step(4)
    prepare_images(mod(z + 4, 8))
    score_band(lax.rem(z, 4), False)

    kept = []
    for e in range(2):
        total = jnp.zeros((16, MASKW), F32)
        for band in range(BANDS):
            slot = mod(y + 4 * e + mod(band - y + 1, 4) - 1, 8)
            total += imgbuf[slot, :, 2 * COEF :].astype(F32)
        kept.append(lax.dot_general(total.astype(BF16), spread, (((1,), (0,)), ((), ())), preferred_element_type=F32))

    lane8 = lax.broadcasted_iota(jnp.int32, (8, 128), 1)
    message = jnp.zeros((8, 128), F32)
    for q in range(4):
        e, block = q // 2, q % 2
        tiles = []
        for dx in range(SIDE):
            line = kept[e][2 * dx + block : 2 * dx + block + 1]
            tiles.append(sbuf[dx * 32 + q * 8 : dx * 32 + q * 8 + 8, :] + norms - PENALTY * (BANDS - line))
        peak = tiles[0]
        for tile in tiles[1:]:
            peak = jnp.maximum(peak, tile)
        peak = jnp.max(peak, axis=1, keepdims=True)
        mass = jnp.zeros((8, ROWS), F32)
        for dx in range(SIDE):
            raised = jnp.exp(tiles[dx] - peak)
            sbuf[dx * 32 + q * 8 : dx * 32 + q * 8 + 8, :] = raised
            mass += raised
        mass = jnp.sum(mass, axis=1, keepdims=True)
        message = jnp.where(lane8 == q, peak, jnp.where(lane8 == 4 + q, mass, message))
    zbuf[z] = message

    def z_copy(d):
        return remote(zbuf.at[z], zbuf.at[z], zsend.at[d], zrecv.at[d], dev(y, mod(z + d, 8), x, core))

    def z_arrival(d):
        slot = mod(z - d, 8)
        return remote(zbuf.at[slot], zbuf.at[slot], zsend.at[d], zrecv.at[d], dev(y, slot, x, core))

    @pl.loop(1, 8)
    def _(d):
        z_copy(d).start()

    @pl.loop(1, 8)
    def _(d):
        z_arrival(d).wait_recv()

    top = zbuf[0]
    for slot in range(1, 8):
        top = jnp.maximum(top, zbuf[slot])
    whole = jnp.zeros((8, 128), F32)
    for slot in range(8):
        part = zbuf[slot]
        whole += pltpu.roll(part, 124, 1) * jnp.exp(jnp.where(lane8 < 4, part - top, 0.0))
    factor = jnp.exp(jnp.where(lane8 < 4, message - top, 0.0)) / jnp.where(lane8 < 4, whole, 1.0)
    for q in range(4):
        scale = factor[:, q : q + 1]
        for dx in range(SIDE):
            sbuf[dx * 32 + q * 8 : dx * 32 + q * 8 + 8, :] = sbuf[dx * 32 + q * 8 : dx * 32 + q * 8 + 8, :] * scale
    prob = sbuf[...].T
    post[...] = prob.astype(BF16)
    mass = jnp.sum(prob, axis=1, keepdims=True)
    totals = mass[0:32]
    for dy in range(1, SIDE):
        totals += mass[dy * 32 : dy * 32 + 32]
    thi = totals.astype(BF16).astype(F32)
    lane32 = lax.broadcasted_iota(jnp.int32, (32, 128), 1)
    spare_re = jnp.where(lane32 == 0, thi, jnp.where(lane32 == 1, totals - thi, 0.0))
    spare_im = jnp.zeros((32, 128), F32)

    def sums_tile(band, t):
        lanes = pl.ds(pl.multiple_of(t * 128, 128), 128)
        both = pl.ds(pl.multiple_of(t * 256, 256), 256)
        g = jnp.dot(post[...], xbuf[band, :, both], preferred_element_type=F32)
        table = tab[BANDS + band, :, lanes]

        def part(n):
            r = (HALF + n) * 32
            return g[r : r + 32, :128], g[r : r + 32, 128:]

        re, im = part(0)
        for d in range(1, HALF + 1):
            c, s = table[2 * d - 2 : 2 * d - 1], table[2 * d - 1 : 2 * d]
            (ur, ui), (dr, di) = part(d), part(-d)
            re = re + c * (ur + dr) - s * (ui - di)
            im = im + s * (ur - dr) + c * (ui + di)
        return re, im

    def pack(band, t, upper, lower):
        lanes = pl.ds(pl.multiple_of(t * 128, 128), 128)
        for xx in range(4):
            for cc in range(2):
                r = xx * 8 + cc * 4
                rows = jnp.concatenate([a[r : r + 4] for a in (*upper, *lower)], axis=0)
                obuf[band, cc, xx, :, lanes] = rows.astype(BF16)

    def core_copy(k):
        band = mod(y + k, 4)
        return remote(obuf.at[band, 1 - core], cbuf.at[k], csend.at[k], crecv.at[k], partner)

    def out_copy(k):
        py, px = plane(k)
        return remote(obuf.at[py, core, px], fbuf.at[k], osend.at[k], orecv.at[k], dev(py, z, px, core))

    def sums_band(k):
        band = mod(y + k, 4)

        @pl.loop(0, SPLIT - 1)
        def _(t):
            pack(band, t, sums_tile(band, t), sums_tile(band, t + SPLIT))

        pack(band, SPLIT - 1, sums_tile(band, SPLIT - 1), (spare_re, spare_im))
        core_copy(k).start()

    def owners_band(k):
        band = mod(y + k, 4)
        core_copy(k).wait_recv()
        for xx in range(4):
            mine = obuf[band, core, xx].astype(F32) + cbuf[k, xx].astype(F32)
            obuf[band, core, xx] = mine.astype(BF16)
        for j in range(4):
            if (4 * k + j) % 16:
                out_copy(4 * k + j).start()

    sums_band(1)
    sums_band(2)
    owners_band(1)
    sums_band(3)
    owners_band(2)
    sums_band(0)
    owners_band(3)
    owners_band(0)

    @pl.loop(1, 16)
    def _(k):
        out_copy(k).wait_recv()

    final = obuf[y, core, x].astype(F32)
    for k in range(1, 16):
        final += fbuf[k].astype(F32)
    out_ref[:, :PACK] = final[0:4]
    out_ref[:, COEF : COEF + PACK] = final[4:8]
    out_ref[:, PACK:COEF] = final[8:12, : COEF - PACK]
    out_ref[:, COEF + PACK :] = final[12:16, : COEF - PACK]
    pair = final[8:12, COEF - PACK : COEF - PACK + 1] + final[8:12, COEF - PACK + 1 : COEF - PACK + 2]
    eye = lax.broadcasted_iota(jnp.int32, (4, 4), 0) == lax.broadcasted_iota(jnp.int32, (4, 4), 1)
    tot_ref[...] = jnp.sum(jnp.where(eye, pair, 0.0), axis=0, keepdims=True)

    @pl.when(moved)
    def _():
        for j in range(5):
            move(j).wait_send()

    for step in range(1, 5):
        for j in RIGHT[step - 1]:
            ring_right(step, j).wait_send()
        for j in LEFT[step - 1]:
            ring_left(step, j).wait_send()

    @pl.loop(1, 16)
    def _(k):
        refs_copy(k).wait_send()
        out_copy(k).wait_send()

    @pl.loop(0, 16)
    def _(k):
        refs_forward(k).wait_send()

    @pl.loop(1, 8)
    def _(d):
        z_copy(d).wait_send()

    @pl.loop(0, 4)
    def _(k):
        core_copy(k).wait_send()


def per_device(images, references, noise_weight, masks):
    vmem = pl.BlockSpec(memory_space=pltpu.VMEM)
    dma = pltpu.SemaphoreType.DMA
    sums, totals = pl.pallas_call(
        kernel,
        out_shape=(jax.ShapeDtypeStruct((4, 2 * COEF), F32), jax.ShapeDtypeStruct((1, 4), F32)),
        in_specs=[pl.BlockSpec(memory_space=pltpu.HBM)] * 5,
        out_specs=(vmem, vmem),
        scratch_shapes=[
            pltpu.VMEM((4, 2 * COEF), BF16),
            pltpu.VMEM((1, COEF), F32),
            pltpu.VMEM((SIDE * SIDE, 2, 64), jnp.int32),
            pltpu.VMEM((2 * BANDS, 8, COEF), F32),
            pltpu.VMEM((16, MASKW), BF16),
            pltpu.VMEM((16, MASKW), F32),
            pltpu.VMEM((8, 16, BLOCK), BF16),
            pltpu.VMEM((16, PACK), F32),
            pltpu.VMEM((BANDS, 4, 2, 16, PACK), BF16),
            pltpu.VMEM((BANDS, ROWS, 2 * COEF), BF16),
            pltpu.VMEM((BANDS, ROWS, 2 * COEF), BF16),
            pltpu.VMEM((ROWS, ROWS), F32),
            pltpu.VMEM((ROWS, ROWS), BF16),
            pltpu.VMEM((8, 8, 128), F32),
            pltpu.VMEM((BANDS, 2, 4, 16, PACK), BF16),
            pltpu.VMEM((BANDS, 4, 16, PACK), BF16),
            pltpu.VMEM((16, 16, PACK), BF16),
            dma((3,)), dma, dma((5,)), dma((5,)),
            dma((4, 4)), dma((4, 4)), dma((4, 4)), dma((4, 4)),
            dma((16,)), dma((16,)), dma((16,)), dma((16,)),
            dma((8,)), dma((8,)), dma((4,)), dma((4,)), dma((16,)), dma((16,)),
        ],
        compiler_params=pltpu.CompilerParams(
            collective_id=0, has_side_effects=True, vmem_limit_bytes=60 * 1024 * 1024
        ),
    )(
        images[0],
        references[0],
        noise_weight,
        jnp.transpose(masks[0], (2, 0, 1)),
        jnp.asarray(trig_tables()),
    )
    return sums[None], totals[0]


def solution(mesh):
    in_specs = (
        P("band", "img", None),
        P("band", "img", None),
        P("band", None),
        P("band", "img", None, None),
    )
    out_specs = (P("band", "img", None), P("img"))
    return jax.shard_map(
        per_device, mesh=mesh, in_specs=in_specs, out_specs=out_specs, check_vma=False
    )
```

```python
import functools
import math

import jax
import jax.numpy as jnp
import numpy as np
from jax import lax
from jax.experimental import pallas as pl
from jax.experimental.pallas import tpu as pltpu
from jax.sharding import PartitionSpec as P

BOX = 256
SIDE = 7
HALF = SIDE // 2
PENALTY = 10000.0
BANDS = 4
COEF = 1664
TILES = COEF // 128
SPLIT = 7
PACK = SPLIT * 128
MASKW = 512
BLOCK = 2 * COEF + MASKW
CHUNKS = ((0, 8), (8, 8), (16, 7), (23, 7))
ROWS = 32 * SIDE
F32 = jnp.float32
BF16 = jnp.bfloat16


def trig_tables():
    index = np.arange(COEF)
    out = np.zeros((2 * BANDS, 8, COEF), np.float32)
    for band in range(BANDS):
        freqs = ((37 * index + 11 * band) % 257 - 128, (61 * index + 29 * band) % 129)
        for axis, freq in enumerate(freqs):
            for d in range(1, HALF + 1):
                angle = ((d * freq) % BOX) * (2.0 * math.pi / BOX)
                out[4 * axis + band, 2 * d - 2] = np.cos(angle)
                out[4 * axis + band, 2 * d - 1] = np.sin(angle)
    return out


def mod(a, n):
    return lax.rem(a + 4 * n, n)


def remote(src, dst, send, recv, device):
    return pltpu.make_async_remote_copy(
        src_ref=src,
        dst_ref=dst,
        send_sem=send,
        recv_sem=recv,
        device_id=device,
        device_id_type=pl.DeviceIdType.MESH,
    )


def nt_dot(a, b):
    return lax.dot_general(a, b, (((1,), (1,)), ((), ())), preferred_element_type=F32)


def kernel(
    images_hbm, refs_hbm, noise_hbm, masks_hbm, tab_hbm,
    out_ref, tot_ref,
    refs_ref, noise_ref, masks_ref, tab, stage, mcat, imgbuf, wpack, rbuf, xbuf, wbuf, sbuf, post, zbuf, obuf, cbuf, fbuf,
    in_sem, tab_sem, tsend, trecv, rsend, rrecv, lsend, lrecv, wsend, wrecv, fsend, frecv,
    zsend, zrecv, csend, crecv, osend, orecv,
):
    y = lax.axis_index("band")
    m = lax.axis_index("img")
    core = lax.rem(m, 2)
    x = lax.rem(m // 2, 4)
    z = m // 8

    def dev(y, z, x, c):
        return (y, (z * 4 + x) * 2 + c)

    to_y = lax.rem(z, 4)
    to_z = mod(z + mod(y - to_y + 1, 4) - 1, 8)
    my_band = lax.rem(z, 4)

    def origin(slot):
        return mod(slot - (mod(lax.rem(slot, 4) - y + 1, 4) - 1), 8)

    moved = to_y != y
    target = dev(to_y, to_z, x, core)
    source = dev(my_band, origin(z), x, core)
    partner = dev(y, z, x, 1 - core)
    zright = dev(y, mod(z + 1, 8), x, core)
    zleft = dev(y, mod(z - 1, 8), x, core)

    def plane(k):
        return mod(y + k // 4, 4), mod(x + lax.rem(k, 4), 4)

    def plane_from(k):
        return mod(y - k // 4, 4), mod(x - lax.rem(k, 4), 4)

    barrier = pltpu.get_barrier_semaphore()

    def signal(device):
        pl.semaphore_signal(barrier, inc=1, device_id=device, device_id_type=pl.DeviceIdType.MESH)

    inputs = [
        pltpu.make_async_copy(refs_hbm, refs_ref, in_sem.at[0]),
        pltpu.make_async_copy(noise_hbm, noise_ref, in_sem.at[1]),
        pltpu.make_async_copy(masks_hbm, masks_ref, in_sem.at[2]),
    ]
    for copy in inputs:
        copy.start()
    tab_copy = pltpu.make_async_copy(tab_hbm, tab, tab_sem)
    tab_copy.start()

    @pl.when(moved)
    def _():
        signal(target)

    apart = mod(y - to_y, 4) == 2

    @pl.when(apart)
    def _():
        signal(source)

    signal(partner)

    @pl.loop(1, 8)
    def _(d):
        signal(dev(y, mod(z + d, 8), x, core))

    @pl.loop(1, 16)
    def _(k):
        py, px = plane(k)
        signal(dev(py, z, px, core))

    pl.semaphore_wait(barrier, 23 + moved.astype(jnp.int32) + apart.astype(jnp.int32))

    def lanes_of(j):
        return pl.ds(CHUNKS[j][0] * 128, CHUNKS[j][1] * 128)

    def piece(j, slot):
        if j == 4:
            return stage, imgbuf.at[slot, :, pl.ds(2 * COEF, MASKW)]
        first = CHUNKS[j][0] * 128
        lanes = pl.ds(first, min(CHUNKS[j][1] * 128, 2 * COEF - first))
        return images_hbm.at[:, lanes], imgbuf.at[slot, :, lanes]

    def move(j):
        return remote(*piece(j, to_z), tsend.at[j], trecv.at[j], target)

    def moved_in(j):
        return remote(*piece(j, z), tsend.at[j], trecv.at[j], source)

    def keep(j):
        return pltpu.make_async_copy(*piece(j, z), tsend.at[j])

    def move_start(j):
        @pl.when(moved)
        def _():
            move(j).start()

        @pl.when(jnp.logical_not(moved))
        def _():
            keep(j).start()

    for j in range(4):
        move_start(j)

    def refs_copy(k):
        py, px = plane(k)
        return remote(rbuf.at[core, y, x], rbuf.at[core, y, x], wsend.at[k], wrecv.at[k], dev(py, z, px, core))

    def refs_arrival(k):
        py, px = plane_from(k)
        return remote(rbuf.at[core, py, px], rbuf.at[core, py, px], wsend.at[k], wrecv.at[k], dev(py, z, px, core))

    def refs_forward(g):
        band = mod(y - g, 4)
        return remote(rbuf.at[core, band], rbuf.at[core, band], fsend.at[g], frecv.at[g], partner)

    def refs_forwarded(g):
        band = mod(y - g, 4)
        return remote(rbuf.at[1 - core, band], rbuf.at[1 - core, band], fsend.at[g], frecv.at[g], partner)

    def refs_group(g):
        for k in range(4 * g, 4 * g + 4):
            if k:
                refs_arrival(k).wait_recv()
        refs_forward(g).start()

    for copy in inputs:
        copy.wait()

    values = refs_ref[...].astype(F32)
    weight = noise_ref[...]
    re, im = values[:, :COEF], values[:, COEF:]
    wre, wim = re * weight, im * weight
    norm = jnp.sum(re * wre + im * wim, axis=1, keepdims=True)
    hi = norm.astype(BF16).astype(F32)
    mid = (norm - hi).astype(BF16).astype(F32)
    low = norm - hi - mid
    lane4 = lax.broadcasted_iota(jnp.int32, (4, 128), 1)
    spare = jnp.where(lane4 == 0, hi, jnp.where(lane4 == 1, mid, jnp.where(lane4 == 2, low, 0.0)))
    wpack[0:4, :] = wre[:, :PACK]
    wpack[4:8, :] = wim[:, :PACK]
    wpack[8:12, : COEF - PACK] = wre[:, PACK:]
    wpack[12:16, : COEF - PACK] = wim[:, PACK:]
    wpack[8:12, COEF - PACK :] = spare
    wpack[12:16, COEF - PACK :] = jnp.zeros((4, 128), F32)
    rbuf[core, y, x] = wpack[...].astype(BF16)

    for k in (10, 11, 14, 15, 2, 8, 9, 6, 5, 7, 13, 12, 4, 3, 1):
        refs_copy(k).start()

    mcat[...] = jnp.zeros_like(mcat)
    for s in range(SIDE * SIDE):
        dx, dy = s // SIDE, s % SIDE
        mcat[2 * dx : 2 * dx + 2, dy * 64 : dy * 64 + 64] = masks_ref[s].astype(F32)
    stage[...] = mcat[...].astype(BF16)

    move_start(4)

    RIGHT = [(0, 1, 2, 3)] * 3 + [(0, 1)]
    LEFT = [(0, 1, 2, 3)] * 3 + [(2, 3)]

    def ring_copy(slot, step, j, send, recv, device):
        ref = imgbuf.at[slot, :, lanes_of(j)]
        return remote(ref, ref, send.at[step - 1, j], recv.at[step - 1, j], device)

    def ring_right(step, j):
        return ring_copy(mod(z - (step - 1), 8), step, j, rsend, rrecv, zright)

    def ring_left(step, j):
        return ring_copy(mod(z + (step - 1), 8), step, j, lsend, lrecv, zleft)

    def ring_step(step, *gaps):
        for j in range(4):
            if j in RIGHT[step - 1]:
                ring_copy(mod(z - step, 8), step, j, rsend, rrecv, zleft).wait_recv()
                if step < 4 and j in RIGHT[step]:
                    ring_right(step + 1, j).start()
            if j in LEFT[step - 1]:
                ring_copy(mod(z + step, 8), step, j, lsend, lrecv, zright).wait_recv()
                if step < 4 and j in LEFT[step]:
                    ring_left(step + 1, j).start()
            for work in gaps[j : j + 1]:
                work()

    for j in range(4):
        for jj in (3, 4) if j == 3 else (j,):

            @pl.when(moved)
            def _():
                moved_in(jj).wait_recv()

            @pl.when(jnp.logical_not(moved))
            def _():
                keep(jj).wait()

        ring_right(1, j).start()
        ring_left(1, j).start()
    tab_copy.wait()

    def shifted(re, im, table, d):
        c, s = table[2 * d - 2 : 2 * d - 1], table[2 * d - 1 : 2 * d]
        a, b, g, h = re * c, im * s, re * s, im * c
        return (a - b, g + h), (a + b, h - g)

    def prepare_images(slot):
        band = lax.rem(slot, 4)
        first = (origin(slot) // 4) * (ROWS // 2)

        def rows(n):
            return pl.ds(pl.multiple_of((HALF + n) * 16 + first, 16), 16)

        @pl.loop(0, TILES)
        def _(t):
            lanes = pl.ds(pl.multiple_of(t * 128, 128), 128)
            lanes_im = pl.ds(pl.multiple_of(t * 128 + COEF, 128), 128)
            out_re = pl.ds(pl.multiple_of(t * 256, 128), 128)
            out_im = pl.ds(pl.multiple_of(t * 256 + 128, 128), 128)
            raw_re, raw_im = imgbuf[slot, :, lanes], imgbuf[slot, :, lanes_im]
            xbuf[band, rows(0), out_re] = raw_re
            xbuf[band, rows(0), out_im] = raw_im
            re, im = raw_re.astype(F32), raw_im.astype(F32)
            table = tab[band, :, lanes]
            for d in range(1, HALF + 1):
                up, down = shifted(re, im, table, d)
                xbuf[band, rows(d), out_re] = up[0].astype(BF16)
                xbuf[band, rows(d), out_im] = up[1].astype(BF16)
                xbuf[band, rows(-d), out_re] = down[0].astype(BF16)
                xbuf[band, rows(-d), out_im] = down[1].astype(BF16)

    def prepare_refs(band):
        def store(t, re, im):
            lanes = pl.ds(pl.multiple_of(t * 128, 128), 128)
            out_re = pl.ds(pl.multiple_of(t * 256, 128), 128)
            out_im = pl.ds(pl.multiple_of(t * 256 + 128, 128), 128)
            table = tab[BANDS + band, :, lanes]

            def put(n, pair):
                wbuf[band, (HALF + n) * 32 : (HALF + n) * 32 + 32, out_re] = pair[0].astype(BF16)
                wbuf[band, (HALF + n) * 32 : (HALF + n) * 32 + 32, out_im] = pair[1].astype(BF16)

            put(0, (re, im))
            for d in range(1, HALF + 1):
                up, down = shifted(re, im, table, d)
                put(-d, up)
                put(d, down)

        def load(t):
            lanes = pl.ds(pl.multiple_of(t * 128, 128), 128)
            blocks = [rbuf[cc, band, xx, :, lanes].astype(F32) for xx in range(4) for cc in range(2)]
            return [jnp.concatenate([b[4 * q : 4 * q + 4] for b in blocks], axis=0) for q in range(4)]

        @pl.loop(0, SPLIT - 1)
        def _(t):
            re, im, re2, im2 = load(t)
            store(t, re, im)
            store(t + SPLIT, re2, im2)

        re, im, spare, _ = load(SPLIT - 1)
        store(SPLIT - 1, re, im)
        return spare

    def score_band(band, first):
        term = nt_dot(xbuf[band], wbuf[band])
        if first:
            sbuf[...] = term
        else:
            sbuf[...] += term

    def score_half(slot):
        band = lax.rem(slot, 4)
        rows = pl.ds(pl.multiple_of((origin(slot) // 4) * (ROWS // 2), 16), ROWS // 2)
        sbuf[rows, :] += nt_dot(xbuf[band, rows, :], wbuf[band])

    prepare_images(z)
    ring_step(1)

    def refs_groups(*groups):
        for g in groups:
            refs_group(g)

    ring_step(
        2,
        lambda: prepare_images(mod(z - 1, 8)),
        lambda: prepare_images(mod(z + 1, 8)),
        lambda: refs_groups(0, 1),
        lambda: refs_groups(2, 3),
    )
    spares = []

    def refs_ready(*groups):
        for g in groups:
            refs_forwarded(g).wait_recv()
            spares.append(prepare_refs(mod(y - g, 4)).astype(BF16))

    prepare_images(mod(z - 2, 8))
    prepare_images(mod(z + 2, 8))
    ring_step(
        3,
        lambda: refs_ready(0),
        lambda: refs_ready(1),
        lambda: refs_ready(2),
        lambda: refs_ready(3),
    )
    score_band(mod(z + 2, 4), True)
    prepare_images(mod(z - 3, 8))
    prepare_images(mod(z + 3, 8))
    score_band(mod(z + 1, 4), False)
    score_band(mod(z + 3, 4), False)
    score_half(z)
    half = jnp.where(lax.broadcasted_iota(jnp.int32, (8, 128), 1) < 3, -0.5, 0.0).astype(BF16)
    norms = jnp.zeros((8, 32), F32)
    for spare in spares:
        norms += nt_dot(half, spare)
    norms = jnp.concatenate([norms] * SIDE, axis=1)
    row = lax.broadcasted_iota(jnp.int32, (MASKW, ROWS), 0)
    lane = lax.broadcasted_iota(jnp.int32, (MASKW, ROWS), 1)
    spread = jnp.where(row == (lane >> 5) * 64 + 8 * z + ((lane & 31) >> 2), 1.0, 0.0).astype(BF16)

    ring_step(4)
    prepare_images(mod(z + 4, 8))
    score_half(mod(z + 4, 8))

    kept = []
    for e in range(2):
        total = jnp.zeros((16, MASKW), F32)
        for band in range(BANDS):
            slot = mod(y + 4 * e + mod(band - y + 1, 4) - 1, 8)
            total += imgbuf[slot, :, 2 * COEF :].astype(F32)
        kept.append(lax.dot_general(total.astype(BF16), spread, (((1,), (0,)), ((), ())), preferred_element_type=F32))

    lane8 = lax.broadcasted_iota(jnp.int32, (8, 128), 1)
    message = jnp.zeros((8, 128), F32)

    def line_of(q, dx):
        first = (q // 2) * (ROWS // 2) + dx * 16 + (q % 2) * 8
        return slice(first, first + 8)

    for q in range(4):
        e, block = q // 2, q % 2
        tiles = []
        for dx in range(SIDE):
            line = kept[e][2 * dx + block : 2 * dx + block + 1]
            tiles.append(sbuf[line_of(q, dx), :] + norms - PENALTY * (BANDS - line))
        peak = tiles[0]
        for tile in tiles[1:]:
            peak = jnp.maximum(peak, tile)
        peak = jnp.max(peak, axis=1, keepdims=True)
        mass = jnp.zeros((8, ROWS), F32)
        for dx in range(SIDE):
            raised = jnp.exp(tiles[dx] - peak)
            sbuf[line_of(q, dx), :] = raised
            mass += raised
        mass = jnp.sum(mass, axis=1, keepdims=True)
        message = jnp.where(lane8 == q, peak, jnp.where(lane8 == 4 + q, mass, message))
    zbuf[z] = message

    def z_copy(d):
        return remote(zbuf.at[z], zbuf.at[z], zsend.at[d], zrecv.at[d], dev(y, mod(z + d, 8), x, core))

    def z_arrival(d):
        slot = mod(z - d, 8)
        return remote(zbuf.at[slot], zbuf.at[slot], zsend.at[d], zrecv.at[d], dev(y, slot, x, core))

    for d in (4, 3, 5, 2, 6, 1, 7):
        z_copy(d).start()
    for d in (1, 7, 2, 6, 3, 5, 4):
        z_arrival(d).wait_recv()

    top = zbuf[0]
    for slot in range(1, 8):
        top = jnp.maximum(top, zbuf[slot])
    whole = jnp.zeros((8, 128), F32)
    for slot in range(8):
        part = zbuf[slot]
        whole += pltpu.roll(part, 124, 1) * jnp.exp(jnp.where(lane8 < 4, part - top, 0.0))
    factor = jnp.exp(jnp.where(lane8 < 4, message - top, 0.0)) / jnp.where(lane8 < 4, whole, 1.0)
    for q in range(4):
        scale = factor[:, q : q + 1]
        for dx in range(SIDE):
            sbuf[line_of(q, dx), :] = sbuf[line_of(q, dx), :] * scale
    prob = sbuf[...].T
    post[...] = prob.astype(BF16)
    mass = jnp.sum(prob, axis=1, keepdims=True)
    totals = mass[0:32]
    for dy in range(1, SIDE):
        totals += mass[dy * 32 : dy * 32 + 32]
    thi = totals.astype(BF16).astype(F32)
    lane32 = lax.broadcasted_iota(jnp.int32, (32, 128), 1)
    spare_re = jnp.where(lane32 == 0, thi, jnp.where(lane32 == 1, totals - thi, 0.0))
    spare_im = jnp.zeros((32, 128), F32)

    def sums_tile(band, t):
        lanes = pl.ds(pl.multiple_of(t * 128, 128), 128)
        both = pl.ds(pl.multiple_of(t * 256, 256), 256)
        g = jnp.dot(post[...], xbuf[band, :, both], preferred_element_type=F32)
        table = tab[BANDS + band, :, lanes]

        def part(n):
            r = (HALF + n) * 32
            return g[r : r + 32, :128], g[r : r + 32, 128:]

        re, im = part(0)
        for d in range(1, HALF + 1):
            c, s = table[2 * d - 2 : 2 * d - 1], table[2 * d - 1 : 2 * d]
            (ur, ui), (dr, di) = part(d), part(-d)
            re = re + c * (ur + dr) - s * (ui - di)
            im = im + s * (ur - dr) + c * (ui + di)
        return re, im

    def pack(band, t, upper, lower):
        lanes = pl.ds(pl.multiple_of(t * 128, 128), 128)
        for xx in range(4):
            for cc in range(2):
                r = xx * 8 + cc * 4
                rows = jnp.concatenate([a[r : r + 4] for a in (*upper, *lower)], axis=0)
                obuf[band, cc, xx, :, lanes] = rows.astype(BF16)

    def core_copy(k):
        band = mod(y + k, 4)
        return remote(obuf.at[band, 1 - core], cbuf.at[k], csend.at[k], crecv.at[k], partner)

    def out_copy(k):
        py, px = plane(k)
        return remote(obuf.at[py, core, px], fbuf.at[k], osend.at[k], orecv.at[k], dev(py, z, px, core))

    def sums_band(k):
        band = mod(y + k, 4)

        @pl.loop(0, SPLIT - 1, unroll=6)
        def _(t):
            pack(band, t, sums_tile(band, t), sums_tile(band, t + SPLIT))

        pack(band, SPLIT - 1, sums_tile(band, SPLIT - 1), (spare_re, spare_im))
        core_copy(k).start()

    def owners_band(k):
        band = mod(y + k, 4)
        core_copy(k).wait_recv()
        for xx in range(4):
            mine = obuf[band, core, xx].astype(F32) + cbuf[k, xx].astype(F32)
            obuf[band, core, xx] = mine.astype(BF16)
        for j in range(4):
            if (4 * k + j) % 16:
                out_copy(4 * k + j).start()

    sums_band(1)
    sums_band(2)
    owners_band(1)
    sums_band(3)
    owners_band(2)
    sums_band(0)
    owners_band(3)
    owners_band(0)

    @pl.loop(1, 16)
    def _(k):
        out_copy(k).wait_recv()

    final = obuf[y, core, x].astype(F32)
    for k in range(1, 16):
        final += fbuf[k].astype(F32)
    out_ref[:, :PACK] = final[0:4]
    out_ref[:, COEF : COEF + PACK] = final[4:8]
    out_ref[:, PACK:COEF] = final[8:12, : COEF - PACK]
    out_ref[:, COEF + PACK :] = final[12:16, : COEF - PACK]
    pair = final[8:12, COEF - PACK : COEF - PACK + 1] + final[8:12, COEF - PACK + 1 : COEF - PACK + 2]
    eye = lax.broadcasted_iota(jnp.int32, (4, 4), 0) == lax.broadcasted_iota(jnp.int32, (4, 4), 1)
    tot_ref[...] = jnp.sum(jnp.where(eye, pair, 0.0), axis=0, keepdims=True)

    @pl.when(moved)
    def _():
        for j in range(5):
            move(j).wait_send()

    for step in range(1, 5):
        for j in RIGHT[step - 1]:
            ring_right(step, j).wait_send()
        for j in LEFT[step - 1]:
            ring_left(step, j).wait_send()

    @pl.loop(1, 16)
    def _(k):
        refs_copy(k).wait_send()
        out_copy(k).wait_send()

    for g in range(4):
        refs_forward(g).wait_send()

    @pl.loop(1, 8)
    def _(d):
        z_copy(d).wait_send()

    @pl.loop(0, 4)
    def _(k):
        core_copy(k).wait_send()


def per_device(images, references, noise_weight, masks):
    vmem = pl.BlockSpec(memory_space=pltpu.VMEM)
    dma = pltpu.SemaphoreType.DMA
    sums, totals = pl.pallas_call(
        kernel,
        out_shape=(jax.ShapeDtypeStruct((4, 2 * COEF), F32), jax.ShapeDtypeStruct((1, 4), F32)),
        in_specs=[pl.BlockSpec(memory_space=pltpu.HBM)] * 5,
        out_specs=(vmem, vmem),
        scratch_shapes=[
            pltpu.VMEM((4, 2 * COEF), BF16),
            pltpu.VMEM((1, COEF), F32),
            pltpu.VMEM((SIDE * SIDE, 2, 64), jnp.int32),
            pltpu.VMEM((2 * BANDS, 8, COEF), F32),
            pltpu.VMEM((16, MASKW), BF16),
            pltpu.VMEM((16, MASKW), F32),
            pltpu.VMEM((8, 16, BLOCK), BF16),
            pltpu.VMEM((16, PACK), F32),
            pltpu.VMEM((2, BANDS, 4, 16, PACK), BF16),
            pltpu.VMEM((BANDS, ROWS, 2 * COEF), BF16),
            pltpu.VMEM((BANDS, ROWS, 2 * COEF), BF16),
            pltpu.VMEM((ROWS, ROWS), F32),
            pltpu.VMEM((ROWS, ROWS), BF16),
            pltpu.VMEM((8, 8, 128), F32),
            pltpu.VMEM((BANDS, 2, 4, 16, PACK), BF16),
            pltpu.VMEM((BANDS, 4, 16, PACK), BF16),
            pltpu.VMEM((16, 16, PACK), BF16),
            dma((3,)), dma, dma((5,)), dma((5,)),
            dma((4, 4)), dma((4, 4)), dma((4, 4)), dma((4, 4)),
            dma((16,)), dma((16,)), dma((4,)), dma((4,)),
            dma((8,)), dma((8,)), dma((4,)), dma((4,)), dma((16,)), dma((16,)),
        ],
        compiler_params=pltpu.CompilerParams(
            collective_id=0, has_side_effects=True, vmem_limit_bytes=60 * 1024 * 1024
        ),
    )(
        images[0],
        references[0],
        noise_weight,
        jnp.transpose(masks[0], (2, 0, 1)),
        jnp.asarray(trig_tables()),
    )
    return sums[None], totals[0]


def solution(mesh):
    in_specs = (
        P("band", "img", None),
        P("band", "img", None),
        P("band", None),
        P("band", "img", None, None),
    )
    out_specs = (P("band", "img", None), P("img"))
    return jax.shard_map(
        per_device, mesh=mesh, in_specs=in_specs, out_specs=out_specs, check_vma=False
    )
```

```python
import functools
import math

import jax
import jax.numpy as jnp
import numpy as np
from jax import lax
from jax.experimental import pallas as pl
from jax.experimental.pallas import tpu as pltpu
from jax.sharding import PartitionSpec as P

BOX = 256
SIDE = 7
HALF = SIDE // 2
PENALTY = 10000.0
BANDS = 4
COEF = 1664
TILES = COEF // 128
SPLIT = 7
PACK = SPLIT * 128
MASKW = 512
CHUNKS = ((0, 5), (5, 4), (9, 4), (13, 5), (18, 4), (22, 4))
PIECES = len(CHUNKS)
ROWS = 32 * SIDE
F32 = jnp.float32
BF16 = jnp.bfloat16


def trig_tables():
    index = np.arange(COEF)
    out = np.zeros((2 * BANDS, 8, COEF), np.float32)
    for band in range(BANDS):
        freqs = ((37 * index + 11 * band) % 257 - 128, (61 * index + 29 * band) % 129)
        for axis, freq in enumerate(freqs):
            for d in range(1, HALF + 1):
                angle = ((d * freq) % BOX) * (2.0 * math.pi / BOX)
                out[4 * axis + band, 2 * d - 2] = np.cos(angle)
                out[4 * axis + band, 2 * d - 1] = np.sin(angle)
    return out


def mod(a, n):
    return lax.rem(a + 4 * n, n)


def remote(src, dst, send, recv, device):
    return pltpu.make_async_remote_copy(
        src_ref=src,
        dst_ref=dst,
        send_sem=send,
        recv_sem=recv,
        device_id=device,
        device_id_type=pl.DeviceIdType.MESH,
    )


def nt_dot(a, b):
    return lax.dot_general(a, b, (((1,), (1,)), ((), ())), preferred_element_type=F32)


def kernel(
    images_hbm, refs_hbm, noise_hbm, masks_hbm, tab_hbm,
    out_ref, tot_ref,
    refs_ref, noise_ref, masks_ref, tab, stage, mcat, mheld, mout, mpart, imgbuf, wpack, rbuf, xbuf, wbuf, sbuf, post, zbuf, obuf, cbuf, fbuf,
    hsend, hrecv, msend, mrecv, in_sem, tab_sem, tsend, trecv, rsend, rrecv, lsend, lrecv, wsend, wrecv, fsend, frecv,
    zsend, zrecv, csend, crecv, osend, orecv,
):
    y = lax.axis_index("band")
    m = lax.axis_index("img")
    core = lax.rem(m, 2)
    x = lax.rem(m // 2, 4)
    z = m // 8

    def dev(y, z, x, c):
        return (y, (z * 4 + x) * 2 + c)

    def way(bands):
        return mod(bands + 1 + core, 4) - 1 - core

    to_y = lax.rem(z, 4)
    to_z = mod(z + way(y - to_y), 8)
    my_band = lax.rem(z, 4)

    def origin(slot):
        return mod(slot - way(lax.rem(slot, 4) - y), 8)

    moved = to_y != y
    target = dev(to_y, to_z, x, core)
    source = dev(my_band, origin(z), x, core)
    partner = dev(y, z, x, 1 - core)
    zright = dev(y, mod(z + 1, 8), x, core)
    zleft = dev(y, mod(z - 1, 8), x, core)

    def plane(k):
        return mod(y + k // 4, 4), mod(x + lax.rem(k, 4), 4)

    def plane_from(k):
        return mod(y - k // 4, 4), mod(x - lax.rem(k, 4), 4)

    barrier = pltpu.get_barrier_semaphore()

    def signal(device):
        pl.semaphore_signal(barrier, inc=1, device_id=device, device_id_type=pl.DeviceIdType.MESH)

    inputs = [
        pltpu.make_async_copy(refs_hbm, refs_ref, in_sem.at[0]),
        pltpu.make_async_copy(noise_hbm, noise_ref, in_sem.at[1]),
        pltpu.make_async_copy(masks_hbm, masks_ref, in_sem.at[2]),
    ]
    for copy in inputs:
        copy.start()
    tab_copy = pltpu.make_async_copy(tab_hbm, tab, tab_sem)
    tab_copy.start()

    @pl.when(moved)
    def _():
        signal(target)

    apart = mod(y - to_y, 4) == 2

    @pl.when(apart)
    def _():
        signal(source)

    signal(partner)

    @pl.loop(1, 8)
    def _(d):
        signal(dev(y, mod(z + d, 8), x, core))

    @pl.loop(1, 16)
    def _(k):
        py, px = plane(k)
        signal(dev(py, z, px, core))

    pl.semaphore_wait(barrier, 23 + moved.astype(jnp.int32) + apart.astype(jnp.int32))

    def lanes_of(j):
        return pl.ds(CHUNKS[j][0] * 128, CHUNKS[j][1] * 128)

    def piece(j, slot):
        return images_hbm.at[:, lanes_of(j)], imgbuf.at[slot, :, lanes_of(j)]

    def move(j):
        return remote(*piece(j, to_z), tsend.at[j], trecv.at[j], target)

    def moved_in(j):
        return remote(*piece(j, z), tsend.at[j], trecv.at[j], source)

    def keep(j):
        return pltpu.make_async_copy(*piece(j, z), tsend.at[j])

    def move_start(j):
        @pl.when(moved)
        def _():
            move(j).start()

        @pl.when(jnp.logical_not(moved))
        def _():
            keep(j).start()

    for j in range(PIECES):
        move_start(j)

    def refs_copy(k):
        py, px = plane(k)
        return remote(rbuf.at[core, y, x], rbuf.at[core, y, x], wsend.at[k], wrecv.at[k], dev(py, z, px, core))

    def refs_arrival(k):
        py, px = plane_from(k)
        return remote(rbuf.at[core, py, px], rbuf.at[core, py, px], wsend.at[k], wrecv.at[k], dev(py, z, px, core))

    def refs_forward(g):
        band = mod(y - g, 4)
        return remote(rbuf.at[core, band], rbuf.at[core, band], fsend.at[g], frecv.at[g], partner)

    def refs_forwarded(g):
        band = mod(y - g, 4)
        return remote(rbuf.at[1 - core, band], rbuf.at[1 - core, band], fsend.at[g], frecv.at[g], partner)

    def refs_group(g):
        for k in range(4 * g, 4 * g + 4):
            if k:
                refs_arrival(k).wait_recv()
        refs_forward(g).start()

    for copy in inputs:
        copy.wait()

    values = refs_ref[...].astype(F32)
    weight = noise_ref[...]
    re, im = values[:, :COEF], values[:, COEF:]
    wre, wim = re * weight, im * weight
    norm = jnp.sum(re * wre + im * wim, axis=1, keepdims=True)
    hi = norm.astype(BF16).astype(F32)
    mid = (norm - hi).astype(BF16).astype(F32)
    low = norm - hi - mid
    lane4 = lax.broadcasted_iota(jnp.int32, (4, 128), 1)
    spare = jnp.where(lane4 == 0, hi, jnp.where(lane4 == 1, mid, jnp.where(lane4 == 2, low, 0.0)))
    wpack[0:4, :] = wre[:, :PACK]
    wpack[4:8, :] = wim[:, :PACK]
    wpack[8:12, : COEF - PACK] = wre[:, PACK:]
    wpack[12:16, : COEF - PACK] = wim[:, PACK:]
    wpack[8:12, COEF - PACK :] = spare
    wpack[12:16, COEF - PACK :] = jnp.zeros((4, 128), F32)
    rbuf[core, y, x] = wpack[...].astype(BF16)

    for k in (10, 11, 14, 15, 2, 8, 9, 6, 5, 7, 13, 12, 4, 3, 1):
        refs_copy(k).start()

    mcat[...] = jnp.zeros_like(mcat)
    for s in range(SIDE * SIDE):
        dx, dy = s // SIDE, s % SIDE
        mcat[2 * dx : 2 * dx + 2, dy * 64 : dy * 64 + 64] = masks_ref[s].astype(F32)
    stage[...] = mcat[...].astype(BF16)
    home_k = mod(to_y - y, 4)

    def mask_copy(k, device):
        return remote(stage, mheld.at[k - 1], hsend, hrecv.at[k - 1], device)

    @pl.when(moved)
    def _():
        mask_copy(home_k, dev(to_y, z, x, core)).start()

    RIGHT = [tuple(range(PIECES))] * 3 + [tuple(range(PIECES // 2))]
    LEFT = [tuple(range(PIECES))] * 3 + [tuple(range(PIECES // 2, PIECES))]

    def ring_copy(slot, step, j, send, recv, device):
        ref = imgbuf.at[slot, :, lanes_of(j)]
        return remote(ref, ref, send.at[step - 1, j], recv.at[step - 1, j], device)

    def ring_right(step, j):
        return ring_copy(mod(z - (step - 1), 8), step, j, rsend, rrecv, zright)

    def ring_left(step, j):
        return ring_copy(mod(z + (step - 1), 8), step, j, lsend, lrecv, zleft)

    def ring_step(step, *gaps):
        for j in range(PIECES):
            if j in RIGHT[step - 1]:
                ring_copy(mod(z - step, 8), step, j, rsend, rrecv, zleft).wait_recv()
                if step < 4 and j in RIGHT[step]:
                    ring_right(step + 1, j).start()
            if j in LEFT[step - 1]:
                ring_copy(mod(z + step, 8), step, j, lsend, lrecv, zright).wait_recv()
                if step < 4 and j in LEFT[step]:
                    ring_left(step + 1, j).start()
            for work in gaps[j : j + 1]:
                work()

    for j in range(PIECES):

        @pl.when(moved)
        def _():
            moved_in(j).wait_recv()

        @pl.when(jnp.logical_not(moved))
        def _():
            keep(j).wait()

        ring_right(1, j).start()
        ring_left(1, j).start()

    half_of = z // 4

    def mask_part(d):
        slot = mod(z + d, 8)
        return remote(mout.at[slot], mpart.at[half_of], msend.at[d], mrecv.at[half_of], dev(y, slot, x, core))

    def mask_arrival(e):
        return remote(mpart.at[e], mpart.at[e], msend.at[0], mrecv.at[e], dev(y, mod(y + 4 * e, 8), x, core))

    @pl.when(jnp.logical_not(moved))
    def _():
        total = mcat[...]
        for k in range(1, 4):
            mask_copy(k, dev(mod(y - k, 4), z, x, core)).wait_recv()
            total += mheld[k - 1].astype(F32)
        group = lax.broadcasted_iota(jnp.int32, (16, 128), 1) >> 3
        for zd in range(8):
            part = jnp.zeros((16, 128), F32)
            for dy in range(SIDE):
                tile = total[:, (dy // 2) * 128 : (dy // 2) * 128 + 128]
                shift = (dy * 8 - (dy % 2) * 64 - 8 * zd) % 128
                part = jnp.where(group == dy, pltpu.roll(tile, shift, 1) if shift else tile, part)
            mout[zd] = part.astype(BF16)
        mpart[half_of] = mout[z]
        for d in (4, 3, 5, 2, 6, 1, 7):
            mask_part(d).start()

    tab_copy.wait()

    def shifted(re, im, table, d):
        c, s = table[2 * d - 2 : 2 * d - 1], table[2 * d - 1 : 2 * d]
        a, b, g, h = re * c, im * s, re * s, im * c
        return (a - b, g + h), (a + b, h - g)

    def prepare_images(slot):
        band = lax.rem(slot, 4)
        first = (origin(slot) // 4) * (ROWS // 2)

        def rows(n):
            return pl.ds(pl.multiple_of((HALF + n) * 16 + first, 16), 16)

        @pl.loop(0, TILES)
        def _(t):
            lanes = pl.ds(pl.multiple_of(t * 128, 128), 128)
            lanes_im = pl.ds(pl.multiple_of(t * 128 + COEF, 128), 128)
            out_re = pl.ds(pl.multiple_of(t * 256, 128), 128)
            out_im = pl.ds(pl.multiple_of(t * 256 + 128, 128), 128)
            raw_re, raw_im = imgbuf[slot, :, lanes], imgbuf[slot, :, lanes_im]
            xbuf[band, rows(0), out_re] = raw_re
            xbuf[band, rows(0), out_im] = raw_im
            re, im = raw_re.astype(F32), raw_im.astype(F32)
            table = tab[band, :, lanes]
            for d in range(1, HALF + 1):
                up, down = shifted(re, im, table, d)
                xbuf[band, rows(d), out_re] = up[0].astype(BF16)
                xbuf[band, rows(d), out_im] = up[1].astype(BF16)
                xbuf[band, rows(-d), out_re] = down[0].astype(BF16)
                xbuf[band, rows(-d), out_im] = down[1].astype(BF16)

    def prepare_refs(band):
        def store(t, re, im):
            lanes = pl.ds(pl.multiple_of(t * 128, 128), 128)
            out_re = pl.ds(pl.multiple_of(t * 256, 128), 128)
            out_im = pl.ds(pl.multiple_of(t * 256 + 128, 128), 128)
            table = tab[BANDS + band, :, lanes]

            def put(n, pair):
                wbuf[band, (HALF + n) * 32 : (HALF + n) * 32 + 32, out_re] = pair[0].astype(BF16)
                wbuf[band, (HALF + n) * 32 : (HALF + n) * 32 + 32, out_im] = pair[1].astype(BF16)

            put(0, (re, im))
            for d in range(1, HALF + 1):
                up, down = shifted(re, im, table, d)
                put(-d, up)
                put(d, down)

        def load(t):
            lanes = pl.ds(pl.multiple_of(t * 128, 128), 128)
            blocks = [rbuf[cc, band, xx, :, lanes].astype(F32) for xx in range(4) for cc in range(2)]
            return [jnp.concatenate([b[4 * q : 4 * q + 4] for b in blocks], axis=0) for q in range(4)]

        @pl.loop(0, SPLIT - 1)
        def _(t):
            re, im, re2, im2 = load(t)
            store(t, re, im)
            store(t + SPLIT, re2, im2)

        re, im, spare, _ = load(SPLIT - 1)
        store(SPLIT - 1, re, im)
        return spare

    def score_band(band, first):
        term = nt_dot(xbuf[band], wbuf[band])
        if first:
            sbuf[...] = term
        else:
            sbuf[...] += term

    def score_half(slot):
        band = lax.rem(slot, 4)
        rows = pl.ds(pl.multiple_of((origin(slot) // 4) * (ROWS // 2), 16), ROWS // 2)
        sbuf[rows, :] += nt_dot(xbuf[band, rows, :], wbuf[band])

    prepare_images(z)
    ring_step(1)

    def refs_groups(*groups):
        for g in groups:
            refs_group(g)

    ring_step(
        2,
        lambda: prepare_images(mod(z - 1, 8)),
        lambda: prepare_images(mod(z + 1, 8)),
        lambda: refs_groups(0, 1),
        lambda: refs_groups(2, 3),
    )
    spares = []

    def refs_ready(*groups):
        for g in groups:
            refs_forwarded(g).wait_recv()
            spares.append(prepare_refs(mod(y - g, 4)).astype(BF16))

    prepare_images(mod(z - 2, 8))
    prepare_images(mod(z + 2, 8))
    ring_step(
        3,
        lambda: refs_ready(0),
        lambda: refs_ready(1),
        lambda: refs_ready(2),
        lambda: refs_ready(3),
    )
    score_band(mod(z + 2, 4), True)
    prepare_images(mod(z - 3, 8))
    prepare_images(mod(z + 3, 8))
    score_band(mod(z + 1, 4), False)
    score_band(mod(z + 3, 4), False)
    score_half(z)
    half = jnp.where(lax.broadcasted_iota(jnp.int32, (8, 128), 1) < 3, -0.5, 0.0).astype(BF16)
    norms = jnp.zeros((8, 32), F32)
    for spare in spares:
        norms += nt_dot(half, spare)
    norms = jnp.concatenate([norms] * SIDE, axis=1)
    row = lax.broadcasted_iota(jnp.int32, (128, ROWS), 0)
    lane = lax.broadcasted_iota(jnp.int32, (128, ROWS), 1)
    spread = jnp.where(row == (lane >> 5) * 8 + ((lane & 31) >> 2), 1.0, 0.0).astype(BF16)
    kept = []
    for e in range(2):

        @pl.when(z != mod(y + 4 * e, 8))
        def _():
            mask_arrival(e).wait_recv()

        kept.append(jnp.dot(mpart[e], spread, preferred_element_type=F32))

    ring_step(4)
    prepare_images(mod(z + 4, 8))
    score_half(mod(z + 4, 8))

    lane8 = lax.broadcasted_iota(jnp.int32, (8, 128), 1)
    message = jnp.zeros((8, 128), F32)

    def line_of(q, dx):
        first = (q // 2) * (ROWS // 2) + dx * 16 + (q % 2) * 8
        return slice(first, first + 8)

    for q in range(4):
        e, block = q // 2, q % 2
        tiles = []
        for dx in range(SIDE):
            line = kept[e][2 * dx + block : 2 * dx + block + 1]
            tiles.append(sbuf[line_of(q, dx), :] + norms - PENALTY * (BANDS - line))
        peak = tiles[0]
        for tile in tiles[1:]:
            peak = jnp.maximum(peak, tile)
        peak = jnp.max(peak, axis=1, keepdims=True)
        mass = jnp.zeros((8, ROWS), F32)
        for dx in range(SIDE):
            raised = jnp.exp(tiles[dx] - peak)
            sbuf[line_of(q, dx), :] = raised
            mass += raised
        mass = jnp.sum(mass, axis=1, keepdims=True)
        message = jnp.where(lane8 == q, peak, jnp.where(lane8 == 4 + q, mass, message))
    zbuf[z] = message

    def z_copy(d):
        return remote(zbuf.at[z], zbuf.at[z], zsend.at[d], zrecv.at[d], dev(y, mod(z + d, 8), x, core))

    def z_arrival(d):
        slot = mod(z - d, 8)
        return remote(zbuf.at[slot], zbuf.at[slot], zsend.at[d], zrecv.at[d], dev(y, slot, x, core))

    for d in (4, 3, 5, 2, 6, 1, 7):
        z_copy(d).start()
    for d in (1, 7, 2, 6, 3, 5, 4):
        z_arrival(d).wait_recv()

    top = zbuf[0]
    for slot in range(1, 8):
        top = jnp.maximum(top, zbuf[slot])
    whole = jnp.zeros((8, 128), F32)
    for slot in range(8):
        part = zbuf[slot]
        whole += pltpu.roll(part, 124, 1) * jnp.exp(jnp.where(lane8 < 4, part - top, 0.0))
    factor = jnp.exp(jnp.where(lane8 < 4, message - top, 0.0)) / jnp.where(lane8 < 4, whole, 1.0)
    for q in range(4):
        scale = factor[:, q : q + 1]
        for dx in range(SIDE):
            sbuf[line_of(q, dx), :] = sbuf[line_of(q, dx), :] * scale
    prob = sbuf[...].T
    post[...] = prob.astype(BF16)
    mass = jnp.sum(prob, axis=1, keepdims=True)
    totals = mass[0:32]
    for dy in range(1, SIDE):
        totals += mass[dy * 32 : dy * 32 + 32]
    thi = totals.astype(BF16).astype(F32)
    lane32 = lax.broadcasted_iota(jnp.int32, (32, 128), 1)
    spare_re = jnp.where(lane32 == 0, thi, jnp.where(lane32 == 1, totals - thi, 0.0))
    spare_im = jnp.zeros((32, 128), F32)

    def sums_tile(band, t):
        lanes = pl.ds(pl.multiple_of(t * 128, 128), 128)
        both = pl.ds(pl.multiple_of(t * 256, 256), 256)
        g = jnp.dot(post[...], xbuf[band, :, both], preferred_element_type=F32)
        table = tab[BANDS + band, :, lanes]

        def part(n):
            r = (HALF + n) * 32
            return g[r : r + 32, :128], g[r : r + 32, 128:]

        re, im = part(0)
        for d in range(1, HALF + 1):
            c, s = table[2 * d - 2 : 2 * d - 1], table[2 * d - 1 : 2 * d]
            (ur, ui), (dr, di) = part(d), part(-d)
            re = re + c * (ur + dr) - s * (ui - di)
            im = im + s * (ur - dr) + c * (ui + di)
        return re, im

    def pack(band, t, upper, lower):
        lanes = pl.ds(pl.multiple_of(t * 128, 128), 128)
        for xx in range(4):
            for cc in range(2):
                r = xx * 8 + cc * 4
                rows = jnp.concatenate([a[r : r + 4] for a in (*upper, *lower)], axis=0)
                obuf[band, cc, xx, :, lanes] = rows.astype(BF16)

    def core_copy(k):
        band = mod(y + k, 4)
        return remote(obuf.at[band, 1 - core], cbuf.at[k], csend.at[k], crecv.at[k], partner)

    def out_copy(k):
        py, px = plane(k)
        return remote(obuf.at[py, core, px], fbuf.at[k], osend.at[k], orecv.at[k], dev(py, z, px, core))

    def sums_band(k):
        band = mod(y + k, 4)

        @pl.loop(0, SPLIT - 1, unroll=6)
        def _(t):
            pack(band, t, sums_tile(band, t), sums_tile(band, t + SPLIT))

        pack(band, SPLIT - 1, sums_tile(band, SPLIT - 1), (spare_re, spare_im))
        core_copy(k).start()

    def owners_band(k):
        band = mod(y + k, 4)
        core_copy(k).wait_recv()
        for xx in range(4):
            mine = obuf[band, core, xx].astype(F32) + cbuf[k, xx].astype(F32)
            obuf[band, core, xx] = mine.astype(BF16)
        for j in range(4):
            if (4 * k + j) % 16:
                out_copy(4 * k + j).start()

    sums_band(1)
    sums_band(2)
    owners_band(1)
    sums_band(3)
    owners_band(2)
    sums_band(0)
    owners_band(3)
    owners_band(0)

    @pl.loop(1, 16)
    def _(k):
        out_copy(k).wait_recv()

    final = obuf[y, core, x].astype(F32)
    for k in range(1, 16):
        final += fbuf[k].astype(F32)
    out_ref[:, :PACK] = final[0:4]
    out_ref[:, COEF : COEF + PACK] = final[4:8]
    out_ref[:, PACK:COEF] = final[8:12, : COEF - PACK]
    out_ref[:, COEF + PACK :] = final[12:16, : COEF - PACK]
    pair = final[8:12, COEF - PACK : COEF - PACK + 1] + final[8:12, COEF - PACK + 1 : COEF - PACK + 2]
    eye = lax.broadcasted_iota(jnp.int32, (4, 4), 0) == lax.broadcasted_iota(jnp.int32, (4, 4), 1)
    tot_ref[...] = jnp.sum(jnp.where(eye, pair, 0.0), axis=0, keepdims=True)

    @pl.when(moved)
    def _():
        for j in range(PIECES):
            move(j).wait_send()
        mask_copy(home_k, dev(to_y, z, x, core)).wait_send()

    @pl.when(jnp.logical_not(moved))
    def _():
        for d in range(1, 8):
            mask_part(d).wait_send()

    for step in range(1, 5):
        for j in RIGHT[step - 1]:
            ring_right(step, j).wait_send()
        for j in LEFT[step - 1]:
            ring_left(step, j).wait_send()

    @pl.loop(1, 16)
    def _(k):
        refs_copy(k).wait_send()
        out_copy(k).wait_send()

    for g in range(4):
        refs_forward(g).wait_send()

    @pl.loop(1, 8)
    def _(d):
        z_copy(d).wait_send()

    @pl.loop(0, 4)
    def _(k):
        core_copy(k).wait_send()


def per_device(images, references, noise_weight, masks):
    vmem = pl.BlockSpec(memory_space=pltpu.VMEM)
    dma = pltpu.SemaphoreType.DMA
    sums, totals = pl.pallas_call(
        kernel,
        out_shape=(jax.ShapeDtypeStruct((4, 2 * COEF), F32), jax.ShapeDtypeStruct((1, 4), F32)),
        in_specs=[pl.BlockSpec(memory_space=pltpu.HBM)] * 5,
        out_specs=(vmem, vmem),
        scratch_shapes=[
            pltpu.VMEM((4, 2 * COEF), BF16),
            pltpu.VMEM((1, COEF), F32),
            pltpu.VMEM((SIDE * SIDE, 2, 64), jnp.int32),
            pltpu.VMEM((2 * BANDS, 8, COEF), F32),
            pltpu.VMEM((16, MASKW), BF16),
            pltpu.VMEM((16, MASKW), F32),
            pltpu.VMEM((3, 16, MASKW), BF16),
            pltpu.VMEM((8, 16, 128), BF16),
            pltpu.VMEM((2, 16, 128), BF16),
            pltpu.VMEM((8, 16, 2 * COEF), BF16),
            pltpu.VMEM((16, PACK), F32),
            pltpu.VMEM((2, BANDS, 4, 16, PACK), BF16),
            pltpu.VMEM((BANDS, ROWS, 2 * COEF), BF16),
            pltpu.VMEM((BANDS, ROWS, 2 * COEF), BF16),
            pltpu.VMEM((ROWS, ROWS), F32),
            pltpu.VMEM((ROWS, ROWS), BF16),
            pltpu.VMEM((8, 8, 128), F32),
            pltpu.VMEM((BANDS, 2, 4, 16, PACK), BF16),
            pltpu.VMEM((BANDS, 4, 16, PACK), BF16),
            pltpu.VMEM((16, 16, PACK), BF16),
            dma, dma((3,)), dma((8,)), dma((2,)), dma((3,)), dma, dma((PIECES,)), dma((PIECES,)),
            dma((4, PIECES)), dma((4, PIECES)), dma((4, PIECES)), dma((4, PIECES)),
            dma((16,)), dma((16,)), dma((4,)), dma((4,)),
            dma((8,)), dma((8,)), dma((4,)), dma((4,)), dma((16,)), dma((16,)),
        ],
        compiler_params=pltpu.CompilerParams(
            collective_id=0, has_side_effects=True, vmem_limit_bytes=60 * 1024 * 1024
        ),
    )(
        images[0],
        references[0],
        noise_weight,
        jnp.transpose(masks[0], (2, 0, 1)),
        jnp.asarray(trig_tables()),
    )
    return sums[None], totals[0]


def solution(mesh):
    in_specs = (
        P("band", "img", None),
        P("band", "img", None),
        P("band", None),
        P("band", "img", None, None),
    )
    out_specs = (P("band", "img", None), P("img"))
    return jax.shard_map(
        per_device, mesh=mesh, in_specs=in_specs, out_specs=out_specs, check_vma=False
    )
```

```python
import functools
import math

import jax
import jax.numpy as jnp
import numpy as np
from jax import lax
from jax.experimental import pallas as pl
from jax.experimental.pallas import tpu as pltpu
from jax.sharding import PartitionSpec as P

BOX = 256
SIDE = 7
HALF = SIDE // 2
PENALTY = 10000.0
BANDS = 4
COEF = 1664
TILES = COEF // 128
SPLIT = 7
PACK = SPLIT * 128
MASKW = 512
CHUNKS = ((0, 5), (5, 4), (9, 4), (13, 5), (18, 4), (22, 4))
PIECES = len(CHUNKS)
ROWS = 32 * SIDE
F32 = jnp.float32
BF16 = jnp.bfloat16


def trig_tables():
    index = np.arange(COEF)
    out = np.zeros((2 * BANDS, 8, COEF), np.float32)
    for band in range(BANDS):
        freqs = ((37 * index + 11 * band) % 257 - 128, (61 * index + 29 * band) % 129)
        for axis, freq in enumerate(freqs):
            for d in range(1, HALF + 1):
                angle = ((d * freq) % BOX) * (2.0 * math.pi / BOX)
                out[4 * axis + band, 2 * d - 2] = np.cos(angle)
                out[4 * axis + band, 2 * d - 1] = np.sin(angle)
    return out


def mod(a, n):
    return lax.rem(a + 4 * n, n)


def remote(src, dst, send, recv, device):
    return pltpu.make_async_remote_copy(
        src_ref=src,
        dst_ref=dst,
        send_sem=send,
        recv_sem=recv,
        device_id=device,
        device_id_type=pl.DeviceIdType.MESH,
    )


def nt_dot(a, b):
    return lax.dot_general(a, b, (((1,), (1,)), ((), ())), preferred_element_type=F32)


def kernel(
    images_hbm, refs_hbm, noise_hbm, masks_hbm, tab_hbm,
    out_ref, tot_ref,
    refs_ref, noise_ref, masks_ref, tab, stage, mcat, mheld, mout, mpart, imgbuf, wpack, rbuf, xbuf, wbuf, sbuf, post, zbuf, obuf, cbuf, fbuf,
    hsend, hrecv, msend, mrecv, in_sem, tab_sem, tsend, trecv, rsend, rrecv, lsend, lrecv, wsend, wrecv, fsend, frecv,
    zsend, zrecv, csend, crecv, osend, orecv,
):
    y = lax.axis_index("band")
    m = lax.axis_index("img")
    core = lax.rem(m, 2)
    x = lax.rem(m // 2, 4)
    z = m // 8

    def dev(y, z, x, c):
        return (y, (z * 4 + x) * 2 + c)

    def way(bands):
        return mod(bands + 1 + core, 4) - 1 - core

    to_y = lax.rem(z, 4)
    to_z = mod(z + way(y - to_y), 8)
    my_band = lax.rem(z, 4)

    def origin(slot):
        return mod(slot - way(lax.rem(slot, 4) - y), 8)

    moved = to_y != y
    target = dev(to_y, to_z, x, core)
    source = dev(my_band, origin(z), x, core)
    partner = dev(y, z, x, 1 - core)
    zright = dev(y, mod(z + 1, 8), x, core)
    zleft = dev(y, mod(z - 1, 8), x, core)

    def plane(k):
        return mod(y + k // 4, 4), mod(x + lax.rem(k, 4), 4)

    def plane_from(k):
        return mod(y - k // 4, 4), mod(x - lax.rem(k, 4), 4)

    barrier = pltpu.get_barrier_semaphore()

    def signal(device):
        pl.semaphore_signal(barrier, inc=1, device_id=device, device_id_type=pl.DeviceIdType.MESH)

    inputs = [
        pltpu.make_async_copy(refs_hbm, refs_ref, in_sem.at[0]),
        pltpu.make_async_copy(noise_hbm, noise_ref, in_sem.at[1]),
        pltpu.make_async_copy(masks_hbm, masks_ref, in_sem.at[2]),
    ]
    for copy in inputs:
        copy.start()
    tab_copy = pltpu.make_async_copy(tab_hbm, tab, tab_sem)
    tab_copy.start()

    @pl.when(moved)
    def _():
        signal(target)

    apart = mod(y - to_y, 4) == 2

    @pl.when(apart)
    def _():
        signal(source)

    signal(partner)

    @pl.loop(1, 8)
    def _(d):
        signal(dev(y, mod(z + d, 8), x, core))

    @pl.loop(1, 16)
    def _(k):
        py, px = plane(k)
        signal(dev(py, z, px, core))

    pl.semaphore_wait(barrier, 23 + moved.astype(jnp.int32) + apart.astype(jnp.int32))

    def lanes_of(j):
        return pl.ds(CHUNKS[j][0] * 128, CHUNKS[j][1] * 128)

    def piece(j, slot):
        return images_hbm.at[:, lanes_of(j)], imgbuf.at[slot, :, lanes_of(j)]

    def move(j):
        return remote(*piece(j, to_z), tsend.at[j], trecv.at[j], target)

    def moved_in(j):
        return remote(*piece(j, z), tsend.at[j], trecv.at[j], source)

    def keep(j):
        return pltpu.make_async_copy(*piece(j, z), tsend.at[j])

    def move_start(j):
        @pl.when(moved)
        def _():
            move(j).start()

        @pl.when(jnp.logical_not(moved))
        def _():
            keep(j).start()

    for j in range(PIECES):
        move_start(j)

    def refs_copy(k):
        py, px = plane(k)
        return remote(rbuf.at[core, y, x], rbuf.at[core, y, x], wsend.at[k], wrecv.at[k], dev(py, z, px, core))

    def refs_arrival(k):
        py, px = plane_from(k)
        return remote(rbuf.at[core, py, px], rbuf.at[core, py, px], wsend.at[k], wrecv.at[k], dev(py, z, px, core))

    def refs_forward(g):
        band = mod(y - g, 4)
        return remote(rbuf.at[core, band], rbuf.at[core, band], fsend.at[g], frecv.at[g], partner)

    def refs_forwarded(g):
        band = mod(y - g, 4)
        return remote(rbuf.at[1 - core, band], rbuf.at[1 - core, band], fsend.at[g], frecv.at[g], partner)

    def refs_group(g):
        for k in range(4 * g, 4 * g + 4):
            if k:
                refs_arrival(k).wait_recv()
        refs_forward(g).start()

    for copy in inputs:
        copy.wait()

    values = refs_ref[...].astype(F32)
    weight = noise_ref[...]
    re, im = values[:, :COEF], values[:, COEF:]
    wre, wim = re * weight, im * weight
    norm = jnp.sum(re * wre + im * wim, axis=1, keepdims=True)
    hi = norm.astype(BF16).astype(F32)
    mid = (norm - hi).astype(BF16).astype(F32)
    low = norm - hi - mid
    lane4 = lax.broadcasted_iota(jnp.int32, (4, 128), 1)
    spare = jnp.where(lane4 == 0, hi, jnp.where(lane4 == 1, mid, jnp.where(lane4 == 2, low, 0.0)))
    wpack[0:4, :] = wre[:, :PACK]
    wpack[4:8, :] = wim[:, :PACK]
    wpack[8:12, : COEF - PACK] = wre[:, PACK:]
    wpack[12:16, : COEF - PACK] = wim[:, PACK:]
    wpack[8:12, COEF - PACK :] = spare
    wpack[12:16, COEF - PACK :] = jnp.zeros((4, 128), F32)
    rbuf[core, y, x] = wpack[...].astype(BF16)

    for k in (10, 11, 14, 15, 2, 8, 9, 6, 5, 7, 13, 12, 4, 3, 1):
        refs_copy(k).start()

    mcat[...] = jnp.zeros_like(mcat)
    for s in range(SIDE * SIDE):
        dx, dy = s // SIDE, s % SIDE
        mcat[2 * dx : 2 * dx + 2, dy * 64 : dy * 64 + 64] = masks_ref[s].astype(F32)
    stage[...] = mcat[...].astype(BF16)
    home_k = mod(to_y - y, 4)

    def mask_copy(k, device):
        return remote(stage, mheld.at[k - 1], hsend, hrecv.at[k - 1], device)

    @pl.when(moved)
    def _():
        mask_copy(home_k, dev(to_y, z, x, core)).start()

    RIGHT = [tuple(range(PIECES))] * 3 + [tuple(range(PIECES // 2))]
    LEFT = [tuple(range(PIECES))] * 3 + [tuple(range(PIECES // 2, PIECES))]

    def ring_copy(slot, step, j, send, recv, device):
        ref = imgbuf.at[slot, :, lanes_of(j)]
        return remote(ref, ref, send.at[step - 1, j], recv.at[step - 1, j], device)

    def ring_right(step, j):
        return ring_copy(mod(z - (step - 1), 8), step, j, rsend, rrecv, zright)

    def ring_left(step, j):
        return ring_copy(mod(z + (step - 1), 8), step, j, lsend, lrecv, zleft)

    def ring_step(step, *gaps):
        for j in range(PIECES):
            if j in RIGHT[step - 1]:
                ring_copy(mod(z - step, 8), step, j, rsend, rrecv, zleft).wait_recv()
                if step < 4 and j in RIGHT[step]:
                    ring_right(step + 1, j).start()
            if j in LEFT[step - 1]:
                ring_copy(mod(z + step, 8), step, j, lsend, lrecv, zright).wait_recv()
                if step < 4 and j in LEFT[step]:
                    ring_left(step + 1, j).start()
            for work in gaps[j : j + 1]:
                work()

    for j in range(PIECES):

        @pl.when(moved)
        def _():
            moved_in(j).wait_recv()

        @pl.when(jnp.logical_not(moved))
        def _():
            keep(j).wait()

        ring_right(1, j).start()
        ring_left(1, j).start()

    half_of = z // 4

    def mask_part(d):
        slot = mod(z + d, 8)
        return remote(mout.at[slot], mpart.at[half_of], msend.at[d], mrecv.at[half_of], dev(y, slot, x, core))

    def mask_arrival(e):
        return remote(mpart.at[e], mpart.at[e], msend.at[0], mrecv.at[e], dev(y, mod(y + 4 * e, 8), x, core))

    @pl.when(jnp.logical_not(moved))
    def _():
        total = mcat[...]
        for k in range(1, 4):
            mask_copy(k, dev(mod(y - k, 4), z, x, core)).wait_recv()
            total += mheld[k - 1].astype(F32)
        group = lax.broadcasted_iota(jnp.int32, (16, 128), 1) >> 3
        for zd in range(8):
            part = jnp.zeros((16, 128), F32)
            for dy in range(SIDE):
                tile = total[:, (dy // 2) * 128 : (dy // 2) * 128 + 128]
                shift = (dy * 8 - (dy % 2) * 64 - 8 * zd) % 128
                part = jnp.where(group == dy, pltpu.roll(tile, shift, 1) if shift else tile, part)
            mout[zd] = part.astype(BF16)
        mpart[half_of] = mout[z]
        for d in (4, 3, 5, 2, 6, 1, 7):
            mask_part(d).start()

    tab_copy.wait()

    def shifted(re, im, table, d):
        c, s = table[2 * d - 2 : 2 * d - 1], table[2 * d - 1 : 2 * d]
        a, b, g, h = re * c, im * s, re * s, im * c
        return (a - b, g + h), (a + b, h - g)

    def prepare_images(slot):
        band = lax.rem(slot, 4)
        first = (origin(slot) // 4) * (ROWS // 2)

        def rows(n):
            return pl.ds(pl.multiple_of((HALF + n) * 16 + first, 16), 16)

        @pl.loop(0, TILES)
        def _(t):
            lanes = pl.ds(pl.multiple_of(t * 128, 128), 128)
            lanes_im = pl.ds(pl.multiple_of(t * 128 + COEF, 128), 128)
            out_re = pl.ds(pl.multiple_of(t * 256, 128), 128)
            out_im = pl.ds(pl.multiple_of(t * 256 + 128, 128), 128)
            raw_re, raw_im = imgbuf[slot, :, lanes], imgbuf[slot, :, lanes_im]
            xbuf[band, rows(0), out_re] = raw_re
            xbuf[band, rows(0), out_im] = raw_im
            re, im = raw_re.astype(F32), raw_im.astype(F32)
            table = tab[band, :, lanes]
            for d in range(1, HALF + 1):
                up, down = shifted(re, im, table, d)
                xbuf[band, rows(d), out_re] = up[0].astype(BF16)
                xbuf[band, rows(d), out_im] = up[1].astype(BF16)
                xbuf[band, rows(-d), out_re] = down[0].astype(BF16)
                xbuf[band, rows(-d), out_im] = down[1].astype(BF16)

    def prepare_refs(band):
        def store(t, re, im):
            lanes = pl.ds(pl.multiple_of(t * 128, 128), 128)
            out_re = pl.ds(pl.multiple_of(t * 256, 128), 128)
            out_im = pl.ds(pl.multiple_of(t * 256 + 128, 128), 128)
            table = tab[BANDS + band, :, lanes]

            def put(n, pair):
                wbuf[band, (HALF + n) * 32 : (HALF + n) * 32 + 32, out_re] = pair[0].astype(BF16)
                wbuf[band, (HALF + n) * 32 : (HALF + n) * 32 + 32, out_im] = pair[1].astype(BF16)

            put(0, (re, im))
            for d in range(1, HALF + 1):
                up, down = shifted(re, im, table, d)
                put(-d, up)
                put(d, down)

        def load(t):
            lanes = pl.ds(pl.multiple_of(t * 128, 128), 128)
            blocks = [rbuf[cc, band, xx, :, lanes].astype(F32) for xx in range(4) for cc in range(2)]
            return [jnp.concatenate([b[4 * q : 4 * q + 4] for b in blocks], axis=0) for q in range(4)]

        @pl.loop(0, SPLIT - 1)
        def _(t):
            re, im, re2, im2 = load(t)
            store(t, re, im)
            store(t + SPLIT, re2, im2)

        re, im, spare, _ = load(SPLIT - 1)
        store(SPLIT - 1, re, im)
        return spare

    def score_band(band, first):
        term = nt_dot(xbuf[band], wbuf[band])
        if first:
            sbuf[...] = term
        else:
            sbuf[...] += term

    prepare_images(z)
    ring_step(1)

    def refs_groups(*groups):
        for g in groups:
            refs_group(g)

    ring_step(
        2,
        lambda: prepare_images(mod(z - 1, 8)),
        lambda: prepare_images(mod(z + 1, 8)),
        lambda: refs_groups(0, 1),
        lambda: refs_groups(2, 3),
    )
    spares = []

    def refs_ready(*groups):
        for g in groups:
            refs_forwarded(g).wait_recv()
            spares.append(prepare_refs(mod(y - g, 4)).astype(BF16))

    prepare_images(mod(z - 2, 8))
    prepare_images(mod(z + 2, 8))
    ring_step(
        3,
        lambda: refs_ready(0),
        lambda: refs_ready(1),
        lambda: refs_ready(2),
        lambda: refs_ready(3),
    )
    score_band(mod(z + 2, 4), True)
    prepare_images(mod(z - 3, 8))
    prepare_images(mod(z + 3, 8))
    score_band(mod(z + 1, 4), False)
    score_band(mod(z + 3, 4), False)
    half = jnp.where(lax.broadcasted_iota(jnp.int32, (8, 128), 1) < 3, -0.5, 0.0).astype(BF16)
    norms = jnp.zeros((8, 32), F32)
    for spare in spares:
        norms += nt_dot(half, spare)
    norms = jnp.concatenate([norms] * SIDE, axis=1)
    row = lax.broadcasted_iota(jnp.int32, (128, ROWS), 0)
    lane = lax.broadcasted_iota(jnp.int32, (128, ROWS), 1)
    spread = jnp.where(row == (lane >> 5) * 8 + ((lane & 31) >> 2), 1.0, 0.0).astype(BF16)
    kept = []
    for e in range(2):

        @pl.when(z != mod(y + 4 * e, 8))
        def _():
            mask_arrival(e).wait_recv()

        kept.append(jnp.dot(mpart[e], spread, preferred_element_type=F32))

    ring_step(4)
    prepare_images(mod(z + 4, 8))
    score_band(lax.rem(z, 4), False)

    lane8 = lax.broadcasted_iota(jnp.int32, (8, 128), 1)
    message = jnp.zeros((8, 128), F32)

    def line_of(q, dx):
        first = (q // 2) * (ROWS // 2) + dx * 16 + (q % 2) * 8
        return slice(first, first + 8)

    for q in range(4):
        e, block = q // 2, q % 2
        tiles = []
        for dx in range(SIDE):
            line = kept[e][2 * dx + block : 2 * dx + block + 1]
            tiles.append(sbuf[line_of(q, dx), :] + norms - PENALTY * (BANDS - line))
        peak = tiles[0]
        for tile in tiles[1:]:
            peak = jnp.maximum(peak, tile)
        peak = jnp.max(peak, axis=1, keepdims=True)
        mass = jnp.zeros((8, ROWS), F32)
        for dx in range(SIDE):
            raised = jnp.exp(tiles[dx] - peak)
            sbuf[line_of(q, dx), :] = raised
            mass += raised
        mass = jnp.sum(mass, axis=1, keepdims=True)
        message = jnp.where(lane8 == q, peak, jnp.where(lane8 == 4 + q, mass, message))
    zbuf[z] = message

    def z_copy(d):
        return remote(zbuf.at[z], zbuf.at[z], zsend.at[d], zrecv.at[d], dev(y, mod(z + d, 8), x, core))

    def z_arrival(d):
        slot = mod(z - d, 8)
        return remote(zbuf.at[slot], zbuf.at[slot], zsend.at[d], zrecv.at[d], dev(y, slot, x, core))

    for d in (4, 3, 5, 2, 6, 1, 7):
        z_copy(d).start()
    for d in (1, 7, 2, 6, 3, 5, 4):
        z_arrival(d).wait_recv()

    top = zbuf[0]
    for slot in range(1, 8):
        top = jnp.maximum(top, zbuf[slot])
    whole = jnp.zeros((8, 128), F32)
    for slot in range(8):
        part = zbuf[slot]
        whole += pltpu.roll(part, 124, 1) * jnp.exp(jnp.where(lane8 < 4, part - top, 0.0))
    factor = jnp.exp(jnp.where(lane8 < 4, message - top, 0.0)) / jnp.where(lane8 < 4, whole, 1.0)
    for q in range(4):
        scale = factor[:, q : q + 1]
        for dx in range(SIDE):
            sbuf[line_of(q, dx), :] = sbuf[line_of(q, dx), :] * scale
    prob = sbuf[...].T
    post[...] = prob.astype(BF16)
    mass = jnp.sum(prob, axis=1, keepdims=True)
    totals = mass[0:32]
    for dy in range(1, SIDE):
        totals += mass[dy * 32 : dy * 32 + 32]
    thi = totals.astype(BF16).astype(F32)
    lane32 = lax.broadcasted_iota(jnp.int32, (32, 128), 1)
    spare_re = jnp.where(lane32 == 0, thi, jnp.where(lane32 == 1, totals - thi, 0.0))
    spare_im = jnp.zeros((32, 128), F32)

    def sums_tile(band, t):
        lanes = pl.ds(pl.multiple_of(t * 128, 128), 128)
        both = pl.ds(pl.multiple_of(t * 256, 256), 256)
        g = jnp.dot(post[...], xbuf[band, :, both], preferred_element_type=F32)
        table = tab[BANDS + band, :, lanes]

        def part(n):
            r = (HALF + n) * 32
            return g[r : r + 32, :128], g[r : r + 32, 128:]

        re, im = part(0)
        for d in range(1, HALF + 1):
            c, s = table[2 * d - 2 : 2 * d - 1], table[2 * d - 1 : 2 * d]
            (ur, ui), (dr, di) = part(d), part(-d)
            re = re + c * (ur + dr) - s * (ui - di)
            im = im + s * (ur - dr) + c * (ui + di)
        return re, im

    def pack(band, t, upper, lower):
        lanes = pl.ds(pl.multiple_of(t * 128, 128), 128)
        for xx in range(4):
            for cc in range(2):
                r = xx * 8 + cc * 4
                rows = jnp.concatenate([a[r : r + 4] for a in (*upper, *lower)], axis=0)
                obuf[band, cc, xx, :, lanes] = rows.astype(BF16)

    def core_copy(k):
        band = mod(y + k, 4)
        return remote(obuf.at[band, 1 - core], cbuf.at[k], csend.at[k], crecv.at[k], partner)

    def out_copy(k):
        py, px = plane(k)
        return remote(obuf.at[py, core, px], fbuf.at[k], osend.at[k], orecv.at[k], dev(py, z, px, core))

    def sums_band(k):
        band = mod(y + k, 4)

        @pl.loop(0, SPLIT - 1, unroll=6)
        def _(t):
            pack(band, t, sums_tile(band, t), sums_tile(band, t + SPLIT))

        pack(band, SPLIT - 1, sums_tile(band, SPLIT - 1), (spare_re, spare_im))
        core_copy(k).start()

    def owners_band(k):
        band = mod(y + k, 4)
        core_copy(k).wait_recv()
        for xx in range(4):
            mine = obuf[band, core, xx].astype(F32) + cbuf[k, xx].astype(F32)
            obuf[band, core, xx] = mine.astype(BF16)
        for j in range(4):
            if (4 * k + j) % 16:
                out_copy(4 * k + j).start()

    sums_band(1)
    sums_band(2)
    owners_band(1)
    sums_band(3)
    owners_band(2)
    sums_band(0)
    owners_band(3)
    owners_band(0)

    @pl.loop(1, 16)
    def _(k):
        out_copy(k).wait_recv()

    final = obuf[y, core, x].astype(F32)
    for k in range(1, 16):
        final += fbuf[k].astype(F32)
    out_ref[:, :PACK] = final[0:4]
    out_ref[:, COEF : COEF + PACK] = final[4:8]
    out_ref[:, PACK:COEF] = final[8:12, : COEF - PACK]
    out_ref[:, COEF + PACK :] = final[12:16, : COEF - PACK]
    pair = final[8:12, COEF - PACK : COEF - PACK + 1] + final[8:12, COEF - PACK + 1 : COEF - PACK + 2]
    eye = lax.broadcasted_iota(jnp.int32, (4, 4), 0) == lax.broadcasted_iota(jnp.int32, (4, 4), 1)
    tot_ref[...] = jnp.sum(jnp.where(eye, pair, 0.0), axis=0, keepdims=True)

    @pl.when(moved)
    def _():
        for j in range(PIECES):
            move(j).wait_send()
        mask_copy(home_k, dev(to_y, z, x, core)).wait_send()

    @pl.when(jnp.logical_not(moved))
    def _():
        for d in range(1, 8):
            mask_part(d).wait_send()

    for step in range(1, 5):
        for j in RIGHT[step - 1]:
            ring_right(step, j).wait_send()
        for j in LEFT[step - 1]:
            ring_left(step, j).wait_send()

    @pl.loop(1, 16)
    def _(k):
        refs_copy(k).wait_send()
        out_copy(k).wait_send()

    for g in range(4):
        refs_forward(g).wait_send()

    @pl.loop(1, 8)
    def _(d):
        z_copy(d).wait_send()

    @pl.loop(0, 4)
    def _(k):
        core_copy(k).wait_send()


def per_device(images, references, noise_weight, masks):
    vmem = pl.BlockSpec(memory_space=pltpu.VMEM)
    dma = pltpu.SemaphoreType.DMA
    sums, totals = pl.pallas_call(
        kernel,
        out_shape=(jax.ShapeDtypeStruct((4, 2 * COEF), F32), jax.ShapeDtypeStruct((1, 4), F32)),
        in_specs=[pl.BlockSpec(memory_space=pltpu.HBM)] * 5,
        out_specs=(vmem, vmem),
        scratch_shapes=[
            pltpu.VMEM((4, 2 * COEF), BF16),
            pltpu.VMEM((1, COEF), F32),
            pltpu.VMEM((SIDE * SIDE, 2, 64), jnp.int32),
            pltpu.VMEM((2 * BANDS, 8, COEF), F32),
            pltpu.VMEM((16, MASKW), BF16),
            pltpu.VMEM((16, MASKW), F32),
            pltpu.VMEM((3, 16, MASKW), BF16),
            pltpu.VMEM((8, 16, 128), BF16),
            pltpu.VMEM((2, 16, 128), BF16),
            pltpu.VMEM((8, 16, 2 * COEF), BF16),
            pltpu.VMEM((16, PACK), F32),
            pltpu.VMEM((2, BANDS, 4, 16, PACK), BF16),
            pltpu.VMEM((BANDS, ROWS, 2 * COEF), BF16),
            pltpu.VMEM((BANDS, ROWS, 2 * COEF), BF16),
            pltpu.VMEM((ROWS, ROWS), F32),
            pltpu.VMEM((ROWS, ROWS), BF16),
            pltpu.VMEM((8, 8, 128), F32),
            pltpu.VMEM((BANDS, 2, 4, 16, PACK), BF16),
            pltpu.VMEM((BANDS, 4, 16, PACK), BF16),
            pltpu.VMEM((16, 16, PACK), BF16),
            dma, dma((3,)), dma((8,)), dma((2,)), dma((3,)), dma, dma((PIECES,)), dma((PIECES,)),
            dma((4, PIECES)), dma((4, PIECES)), dma((4, PIECES)), dma((4, PIECES)),
            dma((16,)), dma((16,)), dma((4,)), dma((4,)),
            dma((8,)), dma((8,)), dma((4,)), dma((4,)), dma((16,)), dma((16,)),
        ],
        compiler_params=pltpu.CompilerParams(
            collective_id=0, has_side_effects=True, vmem_limit_bytes=60 * 1024 * 1024
        ),
    )(
        images[0],
        references[0],
        noise_weight,
        jnp.transpose(masks[0], (2, 0, 1)),
        jnp.asarray(trig_tables()),
    )
    return sums[None], totals[0]


def solution(mesh):
    in_specs = (
        P("band", "img", None),
        P("band", "img", None),
        P("band", None),
        P("band", "img", None, None),
    )
    out_specs = (P("band", "img", None), P("img"))
    return jax.shard_map(
        per_device, mesh=mesh, in_specs=in_specs, out_specs=out_specs, check_vma=False
    )
```
